256 devices in a mesh: tm: 4 (over x_hi, core), rows: 32 (over z, y), clip: 2 (over x_lo).
Axes of the slice: x: 4 (x_hi: 2, x_lo: 2; x = x_hi * 2 + x_lo), y: 4, z: 8, core: 2. Of those that a mesh axis runs over, the one named last changes fastest.
Arguments:
- video: bfloat16 [2, 16, 64, 128, 384], P('clip', 'tm', 'rows'), may hold values from -8 to 8
- leading_norm_gain: float32 [96], replicated, may hold values from 0.1 to 1.9
- conv_first: bfloat16 [3, 3, 3, 96, 96], replicated, may hold values from -0.125 to 0.125
- strided_down_kernel: bfloat16 [3, 3, 96, 96], replicated, may hold values from -0.21875 to 0.21875
- gain_second: float32 [96], replicated, may hold values from 0.1 to 1.9
- conv_second: bfloat16 [3, 3, 3, 96, 192], replicated, may hold values from -0.125 to 0.125
- shortcut: bfloat16 [96, 192], replicated, may hold values from -0.625 to 0.625
Outputs:
- latents: bfloat16 [2, 16, 32, 64, 768], P(None, 'tm', None, ('rows', 'clip'))
The draws below stay inside these ranges and needn't reach their ends.
All inputs are finite; a program needn't handle non-finite values.
Results may differ from the reference program's by a relative error of at most 0.0058.
Values may be sent and summed in bfloat16 or wider, within the bound.
A program may use at most 128 MiB of HBM per device.

```python
import math
import jax
import jax.numpy as jnp
from jax import lax

C1 = 96
C2 = 192
COLS = 512
CLIPS = 2
FRAMES = 16
HEIGHT = 64


def draw_video(key, part):
    key = jax.random.fold_in(key, 11)
    key_base, key_rough, key_column = jax.random.split(key, 3)
    shape = (CLIPS, FRAMES, HEIGHT, COLS, C1)
    base = jax.random.normal(key_base, shape, jnp.float32)
    ramp = jnp.exp(math.log(3.0) * jnp.arange(HEIGHT, dtype=jnp.float32) / HEIGHT)
    rough = jnp.exp(jax.random.uniform(key_rough, (CLIPS, FRAMES, HEIGHT), jnp.float32, -0.5, 0.5))
    column = jnp.exp(jax.random.uniform(key_column, (COLS,), jnp.float32, -0.8, 0.8))
    value = base * (ramp * rough)[:, :, :, None, None] * column[:, None]
    value = jnp.clip(value, -8.0, 8.0).reshape(CLIPS, FRAMES, HEIGHT, COLS // 4, 4 * C1)
    return value.astype(jnp.bfloat16)


def scatter_about(own_key, dims, deviation, bound, kind=jnp.bfloat16):
    array = deviation * jax.random.normal(own_key, dims, jnp.float32)
    return jnp.clip(array, min=-bound, max=bound).astype(kind)


def setup_inputs(seed: int = 0) -> dict:
    seeds = jax.random.split(jax.random.key(seed), 8)
    video = draw_video(jax.random.fold_in(seeds[7], 71), 0)
    leading_norm_gain = jnp.clip(1.0 + 0.18 * jax.random.normal(seeds[1], (C1,), jnp.float32), 0.1, 1.9)
    conv_first = scatter_about(seeds[2], (3, 3, 3, C1, C1), (27 * C1) ** -0.5, 0.125)
    strided_down_kernel = scatter_about(seeds[3], (3, 3, C1, C1), (9 * C1) ** -0.5, 0.21875)
    gain_second = jnp.clip(1.0 + 0.18 * jax.random.normal(seeds[4], (C1,), jnp.float32), 0.1, 1.9)
    conv_second = scatter_about(seeds[5], (3, 3, 3, C1, C2), (27 * C1) ** -0.5, 0.125)
    shortcut = scatter_about(seeds[6], (C1, C2), C1 ** -0.5, 0.625)
    return {"video": video, "leading_norm_gain": leading_norm_gain, "conv_first": conv_first, "strided_down_kernel": strided_down_kernel, "gain_second": gain_second, "conv_second": conv_second, "shortcut": shortcut}


def norm_silu(receptive_span, gain):
    values = receptive_span.astype(jnp.float32)
    meansq = lax.optimization_barrier(jnp.mean(values * values, axis=-1, keepdims=True))
    scaled = values * lax.rsqrt(meansq + 1e-06) * gain
    return jax.nn.silu(scaled).astype(jnp.bfloat16)

def causal_conv(receptive_span, weight_tensor):
    frames, height, columns, channels = receptive_span.shape
    padded = jnp.pad(receptive_span, ((2, 0), (1, 1), (1, 1), (0, 0)))
    totals = jnp.zeros((frames * height * columns, weight_tensor.shape[-1]), jnp.float32)
    for frame_offset in range(3):
        for row_off in range(3):
            for col_off in range(3):
                window = padded[frame_offset:frame_offset + frames, row_off:row_off + height, col_off:col_off + columns]
                totals = totals + jnp.dot(window.reshape(-1, channels), weight_tensor[frame_offset, row_off, col_off], preferred_element_type=jnp.float32)
    return totals.reshape(frames, height, columns, weight_tensor.shape[-1])

def spatial_halving(receptive_span, weight_tensor):
    frames, height, columns, channels = receptive_span.shape
    half_rows = height // 2
    half_cols = columns // 2
    padded = jnp.pad(receptive_span, ((0, 0), (0, 1), (0, 1), (0, 0)))
    totals = jnp.zeros((frames * half_rows * half_cols, channels), jnp.float32)
    for row_off in range(3):
        for col_off in range(3):
            window = padded[:, row_off:row_off + 2 * half_rows:2, col_off:col_off + 2 * half_cols:2]
            totals = totals + jnp.dot(window.reshape(-1, channels), weight_tensor[row_off, col_off], preferred_element_type=jnp.float32)
    return totals.reshape(frames, half_rows, half_cols, channels).astype(jnp.bfloat16)

def reference(video, leading_norm_gain, conv_first, strided_down_kernel, gain_second, conv_second, shortcut):

    def one_clip(grouped_span):
        frames, height, groups, lane_count = grouped_span.shape
        channels = lane_count // 4
        receptive_span = grouped_span.reshape(frames, height, groups * 4, channels)
        first_norm = norm_silu(receptive_span, leading_norm_gain)
        encoder_segment = (receptive_span.astype(jnp.float32) + causal_conv(first_norm, conv_first)).astype(jnp.bfloat16)
        contracted_result = spatial_halving(encoder_segment, strided_down_kernel)
        second = norm_silu(contracted_result, gain_second)
        mixed_out = causal_conv(second, conv_second)
        skipped = jnp.dot(contracted_result.reshape(-1, contracted_result.shape[-1]), shortcut, preferred_element_type=jnp.float32)
        result = (mixed_out + skipped.reshape(mixed_out.shape)).astype(jnp.bfloat16)
        return result.reshape(frames, height // 2, groups * 4 // 8, 4 * shortcut.shape[-1])
    return lax.map(one_clip, video)
```

```python
import functools

import jax
import jax.numpy as jnp
from jax import lax
from jax.experimental import pallas as pl
from jax.experimental.pallas import tpu as pltpu
from jax.sharding import PartitionSpec as P

MESH = pl.DeviceIdType.MESH
F32 = jnp.float32
BF16 = jnp.bfloat16
VMEM_LIMIT = 56 * 1024 * 1024


def iota2(shape, dim):
    return lax.broadcasted_iota(jnp.int32, shape, dim)


def selector(rows, cols, offset):
    return jnp.where(iota2((rows, cols), 1) == iota2((rows, cols), 0) + offset, 1.0, 0.0).astype(BF16)


def dot(a, b):
    return jnp.dot(a, b, preferred_element_type=F32)


def place_exact(vector, chosen):
    wide = jnp.broadcast_to(vector, (8, vector.shape[1]))
    high = wide.astype(BF16)
    rest = wide - high.astype(F32)
    middle = rest.astype(BF16)
    low = (rest - middle.astype(F32)).astype(BF16)
    return (dot(high, chosen) + dot(middle, chosen) + dot(low, chosen))[0:1]


def squares_split(values):
    square = values * values
    high = square.astype(BF16)
    low = (square - high.astype(F32)).astype(BF16)
    return high, low


def normsilu(values, meansq, gain):
    scaled = values * lax.rsqrt(meansq + 1e-6) * gain
    return scaled / (1.0 + jnp.exp(-scaled))


def shift_down(x):
    moved = pltpu.roll(x, 1, 0)
    return jnp.where(iota2(x.shape, 0) == 0, 0.0, moved)


def shift_up(x):
    rows = x.shape[0]
    moved = pltpu.roll(x, rows - 1, 0)
    return jnp.where(iota2(x.shape, 0) == rows - 1, 0.0, moved)


def section_kernel(
    row_total, tm_total,
    video, gain, w1, wd,
    message,
    first, sides, resid, wa, wb, wda, wdb, section, part_out, part_in, reduced, spread,
    send, recv,
):
    tm = lax.axis_index("tm")
    row = lax.axis_index("rows")
    clip = lax.axis_index("clip")
    has_up, has_down = row > 0, row < row_total - 1
    has_past, has_next = tm > 0, tm < tm_total - 1
    up, down = (tm, row - 1, clip), (tm, row + 1, clip)
    past, after = (tm - 1, row, clip), (tm + 1, row, clip)

    barrier = pltpu.get_barrier_semaphore()
    for exists, who in ((has_up, up), (has_down, down), (has_past, past), (has_next, after)):
        @pl.when(exists)
        def _():
            pl.semaphore_signal(barrier, inc=1, device_id=who, device_id_type=MESH)

    def remote(src, dst, index, who):
        return pltpu.make_async_remote_copy(
            src_ref=src, dst_ref=dst, send_sem=send.at[index], recv_sem=recv.at[index],
            device_id=who, device_id_type=MESH)

    lanes = 384
    ones = jnp.where(
        iota2((lanes, lanes), 0) // 96 == iota2((lanes, lanes), 1) // 96, 1.0, 0.0).astype(BF16)
    spot = iota2((128, 128), 0)
    order = jnp.where(
        iota2((128, 128), 1) == jnp.where(spot < 64, 2 * spot, 2 * spot - 127), 1.0, 0.0).astype(BF16)
    chosen = jnp.where(iota2((96, lanes), 1) % 96 == iota2((96, lanes), 0), 1.0, 0.0).astype(BF16)
    gain_lanes = place_exact(gain[...], chosen)

    def norm_step(index, carry):
        t, r = index // 2, index % 2
        values = dot(order, video[t, r])
        resid[t, r] = values.astype(BF16)
        high, low = squares_split(values)
        meansq = (dot(high, ones) + dot(low, ones)) * (1.0 / 96.0)
        first[t + 2, r + 1] = normsilu(values, meansq, gain_lanes).astype(BF16)
        return carry

    lax.fori_loop(0, 8, norm_step, 0)

    count = has_up.astype(jnp.int32) + has_down.astype(jnp.int32) + has_past.astype(jnp.int32) + has_next.astype(jnp.int32)
    pl.semaphore_wait(barrier, count)

    down_late = remote(first.at[4:6, 2], first.at[4:6, 0], 0, down)
    down_early = remote(first.at[2:4, 2], first.at[2:4, 0], 1, down)
    up_late = remote(first.at[4:6, 1], first.at[4:6, 3], 2, up)
    up_early = remote(first.at[2:4, 1], first.at[2:4, 3], 3, up)
    frames = remote(first.at[4:6, 1:3], first.at[0:2, 1:3], 4, after)
    corner_top = remote(first.at[4:6, 0], first.at[0:2, 0], 5, after)
    corner_low = remote(first.at[4:6, 3], first.at[0:2, 3], 6, after)
    partial = remote(part_out, part_in, 7, up)
    later = remote(reduced.at[4:6], reduced.at[0:2], 8, after)

    @pl.when(has_down)
    def _():
        down_late.start()

    @pl.when(has_up)
    def _():
        up_late.start()

    @pl.when(has_next)
    def _():
        frames.start()

    @pl.when(has_down)
    def _():
        down_early.start()

    @pl.when(has_up)
    def _():
        up_early.start()

    @pl.when(jnp.logical_not(has_up))
    def _():
        first[:, 0] = jnp.zeros((6, 128, 384), BF16)

    @pl.when(jnp.logical_not(has_down))
    def _():
        first[:, 3] = jnp.zeros((6, 128, 384), BF16)

    @pl.when(jnp.logical_not(has_past))
    def _():
        first[0:2, 1:3] = jnp.zeros((2, 2, 128, 384), BF16)
        reduced[0:2] = jnp.zeros((2, 64, 384), BF16)

        @pl.when(has_up)
        def _():
            first[0:2, 0] = jnp.zeros((2, 128, 384), BF16)

        @pl.when(has_down)
        def _():
            first[0:2, 3] = jnp.zeros((2, 128, 384), BF16)

    lane = iota2((96, 1024), 1)
    source = iota2((96, 1024), 0)
    offset = jnp.where(lane < 256, 0, jnp.where(lane < 512, 256 + 96, jnp.where(lane < 768, 512 + 64, 768 + 160)))
    places = jnp.where(lane == source + offset, 1.0, 0.0).astype(BF16)

    def weight_step(tap, carry):
        placed = dot(w1[tap], places)
        a0, a1 = placed[:, 0:256], placed[:, 256:512]
        b0, b1 = placed[:, 512:768], placed[:, 768:1024]
        wa[tap, 0:96] = (a0[96:192] + a1[0:96]).astype(BF16)
        wa[tap, 96:192] = (a0[192:288] + a1[96:192]).astype(BF16)
        wa[tap, 192:288] = a1[192:288].astype(BF16)
        wa[tap, 288:384] = a0[0:96].astype(BF16)
        wb[tap, 0:96] = b1[192:288].astype(BF16)
        wb[tap, 96:192] = b0[0:96].astype(BF16)
        wb[tap, 192:288] = (b0[96:192] + b1[0:96]).astype(BF16)
        wb[tap, 288:384] = (b0[192:288] + b1[96:192]).astype(BF16)
        return carry

    lax.fori_loop(0, 9, weight_step, 0)

    def down_weight_step(tap, carry):
        placed = dot(wd[tap], places)
        for ref, base in ((wda, 0), (wdb, 512)):
            p0, p1 = placed[:, base:base + 256], placed[:, base + 256:base + 512]
            ref[tap, 0:96] = p0[0:96].astype(BF16)
            ref[tap, 96:192] = p0[96:192].astype(BF16)
            ref[tap, 192:288] = (p0[192:288] + p1[0:96]).astype(BF16)
            ref[tap, 288:384] = p1[96:192].astype(BF16)
            ref[tap, 384:480] = p1[192:288].astype(BF16)
            ref[tap, 480:512] = jnp.zeros((32, 256), BF16)
        return carry

    lax.fori_loop(0, 3, down_weight_step, 0)

    @pl.when(has_up)
    def _():
        down_late.wait_recv()

        @pl.when(has_next)
        def _():
            corner_top.start()

    @pl.when(has_down)
    def _():
        up_late.wait_recv()

        @pl.when(has_next)
        def _():
            corner_low.start()

    @pl.when(has_up)
    def _():
        down_early.wait_recv()

    @pl.when(has_down)
    def _():
        up_early.wait_recv()

    @pl.when(has_past)
    def _():
        frames.wait_recv()

        @pl.when(has_up)
        def _():
            corner_top.wait_recv()

        @pl.when(has_down)
        def _():
            corner_low.wait_recv()

    lane64 = iota2((64, 128), 1)

    def side_step(index, carry):
        t, r = index // 4, index % 4
        e0 = first[t, r, 0:64, 0:128].astype(F32)
        o0 = first[t, r, 64:128, 0:128].astype(F32)
        e2 = first[t, r, 0:64, 256:384].astype(F32)
        o2 = first[t, r, 64:128, 256:384].astype(F32)
        sides[0, t, r, 0:64] = jnp.where(lane64 < 32, e2, shift_down(o2)).astype(BF16)
        sides[0, t, r, 64:128] = jnp.where(lane64 < 32, o2, e2).astype(BF16)
        sides[1, t, r, 0:64] = jnp.where(lane64 < 96, o0, e0).astype(BF16)
        sides[1, t, r, 64:128] = jnp.where(lane64 < 96, shift_up(e0), o0).astype(BF16)
        return carry

    lax.fori_loop(0, 24, side_step, 0)

    def conv_step(step, carry):
        t = (step + 2) % 4
        acc_a = jnp.zeros((256, 256), F32)
        acc_b = jnp.zeros((256, 256), F32)
        for a in range(3):
            left, right = [], []
            for i in range(3):
                left += [
                    first[t + a, i:i + 2, :, 0:256].reshape(256, 256),
                    sides[0, t + a, i:i + 2].reshape(256, 128)]
                right += [
                    sides[1, t + a, i:i + 2].reshape(256, 128),
                    first[t + a, i:i + 2, :, 128:384].reshape(256, 256)]
            acc_a += dot(jnp.concatenate(left, 1), wa[3 * a:3 * a + 3].reshape(1152, 256))
            acc_b += dot(jnp.concatenate(right, 1), wb[3 * a:3 * a + 3].reshape(1152, 256))
        out = jnp.concatenate(
            [acc_a[:, 0:128], acc_a[:, 128:256] + acc_b[:, 0:128], acc_b[:, 128:256]], 1)
        total = out + resid[t].reshape(256, 384).astype(F32)
        section[t] = total.astype(BF16).reshape(2, 128, 384)
        return carry

    lax.fori_loop(0, 4, conv_step, 0)

    def down_rows(t, r):
        even = section[t, r, 0:64]
        odd = section[t, r, 64:128]
        following = shift_up(even[:, 0:128].astype(F32)).astype(BF16)
        return jnp.concatenate([even, odd[:, 0:128]], 1), jnp.concatenate([odd, following], 1)

    def merge(a, b):
        return jnp.concatenate([a[:, 0:128], a[:, 128:256] + b[:, 0:128], b[:, 128:256]], 1)

    def partial_step(t, carry):
        left, right = down_rows(t, 0)
        part_out[t] = merge(dot(left, wda[2]), dot(right, wdb[2])).astype(BF16)
        return carry

    lax.fori_loop(0, 4, partial_step, 0)

    @pl.when(has_up)
    def _():
        partial.start()

    @pl.when(has_down)
    def _():
        partial.wait_recv()

    @pl.when(jnp.logical_not(has_down))
    def _():
        part_in[...] = jnp.zeros((4, 64, 384), BF16)

    def down_step(t, carry):
        left0, right0 = down_rows(t, 0)
        left1, right1 = down_rows(t, 1)
        a = dot(left0, wda[0]) + dot(left1, wda[1])
        b = dot(right0, wdb[0]) + dot(right1, wdb[1])
        reduced[t + 2] = (merge(a, b) + part_in[t].astype(F32)).astype(BF16)
        return carry

    lax.fori_loop(0, 4, down_step, 0)

    @pl.when(has_next)
    def _():
        later.start()

    @pl.when(has_past)
    def _():
        later.wait_recv()

    def message_step(t, carry):
        t0 = reduced[t, :, 0:128].astype(F32)
        t1 = reduced[t, :, 128:256].astype(F32)
        t2 = reduced[t, :, 256:384].astype(F32)
        tiles = (t0, t1, t2,
                 jnp.where(lane64 < 32, t2, shift_down(t2)),
                 jnp.where(lane64 < 96, shift_up(t0), t0))
        for j, tile in enumerate(tiles):
            spread[pl.ds(t * 5 + j, 64, stride=32), :] = tile
        return carry

    lax.fori_loop(0, 6, message_step, 0)
    for j in (30, 31):
        spread[pl.ds(j, 64, stride=32), :] = jnp.zeros((64, 128), F32)

    def pack_step(j, carry):
        message[pl.ds(j * 8, 8)] = spread[pl.ds(j * 256, 256), :].astype(BF16).reshape(8, 32, 128)
        return carry

    lax.fori_loop(0, 8, pack_step, 0)

    @pl.when(has_down)
    def _():
        down_late.wait_send()
        down_early.wait_send()

    @pl.when(has_up)
    def _():
        up_late.wait_send()
        up_early.wait_send()
        partial.wait_send()

    @pl.when(has_next)
    def _():
        frames.wait_send()
        later.wait_send()

        @pl.when(has_up)
        def _():
            corner_top.wait_send()

        @pl.when(has_down)
        def _():
            corner_low.wait_send()


def latent_kernel(
    row_total, clip_total,
    message, gain, w2, shortcut,
    out,
    landed, wide, tiles, windows, raw, wa, wb, wsa, wsb, send, recv, own,
):
    tm = lax.axis_index("tm")
    me = lax.axis_index("rows") * clip_total + lax.axis_index("clip")
    total = row_total * clip_total

    def who(index):
        return (tm, index // clip_total, index % clip_total)

    barrier = pltpu.get_barrier_semaphore()

    def greet(step, carry):
        pl.semaphore_signal(barrier, inc=1, device_id=who((me + step) % total), device_id_type=MESH)
        return carry

    lax.fori_loop(1, total, greet, 0)
    mine = pltpu.make_async_copy(message.at[me], landed.at[me], own)
    mine.start()
    pl.semaphore_wait(barrier, total - 1)

    def outgoing(step):
        other = (me + step) % total
        return pltpu.make_async_remote_copy(
            src_ref=message.at[other], dst_ref=landed.at[me],
            send_sem=send.at[step], recv_sem=recv.at[step],
            device_id=who(other), device_id_type=MESH)

    def incoming(step):
        other = (me - step + total) % total
        return pltpu.make_async_remote_copy(
            src_ref=message.at[other], dst_ref=landed.at[other],
            send_sem=send.at[step], recv_sem=recv.at[step],
            device_id=who(other), device_id_type=MESH)

    def start_step(step, carry):
        outgoing(step).start()
        return carry

    lax.fori_loop(1, total, start_step, 0)

    lane = iota2((192, 768), 1)
    source = iota2((192, 768), 0)
    places = jnp.where(lane == jnp.where(lane < 384, source, source + 576), 1.0, 0.0).astype(BF16)

    def weight_step(tap, carry):
        placed = dot(w2[tap], places)
        p0, p1 = placed[:, 0:384], placed[:, 384:768]
        wa[tap, 0:96] = (p0[96:192] + p1[0:96]).astype(BF16)
        wa[tap, 96:192] = (p0[192:288] + p1[96:192]).astype(BF16)
        wa[tap, 192:288] = p1[192:288].astype(BF16)
        wa[tap, 288:384] = p0[0:96].astype(BF16)
        wb[tap, 0:96] = p1[192:288].astype(BF16)
        wb[tap, 96:192] = p0[0:96].astype(BF16)
        wb[tap, 192:288] = (p0[96:192] + p1[0:96]).astype(BF16)
        wb[tap, 288:384] = (p0[192:288] + p1[96:192]).astype(BF16)
        return carry

    lax.fori_loop(0, 9, weight_step, 0)
    placed = dot(shortcut[...], places).astype(BF16)
    q0, q1 = placed[:, 0:384], placed[:, 384:768]
    wsa[0:96] = q0
    wsa[96:192] = q1
    wsa[192:384] = jnp.zeros((192, 384), BF16)
    wsb[0:192] = jnp.zeros((192, 384), BF16)
    wsb[192:288] = q0
    wsb[288:384] = q1

    def group_of(lane_index):
        main = lane_index // 96
        left = jnp.where(lane_index < 416, 2, 4)
        right = jnp.where(lane_index < 608, 5, 1)
        return jnp.where(lane_index < 384, main, jnp.where(lane_index < 512, left, right))

    def channel_of(lane_index):
        main = lane_index % 96
        left = jnp.where(lane_index < 416, lane_index - 384 + 64, lane_index - 416)
        right = jnp.where(lane_index < 608, lane_index - 512, lane_index - 608)
        return jnp.where(lane_index < 384, main, jnp.where(lane_index < 512, left, right))

    rows640 = iota2((640, 640), 0)
    twice = jnp.logical_or(
        jnp.logical_and(rows640 >= 384, rows640 < 416), rows640 >= 608)
    from_group = jnp.where(twice, -1, group_of(rows640))
    ones = jnp.where(from_group == group_of(iota2((640, 640), 1)), 1.0, 0.0).astype(BF16)
    chosen = jnp.where(
        channel_of(iota2((96, 640), 1)) == iota2((96, 640), 0), 1.0, 0.0).astype(BF16)
    gain_lanes = place_exact(gain[...], chosen)

    mine.wait()

    def wait_step(step, carry):
        incoming(step).wait_recv()
        return carry

    lax.fori_loop(1, total, wait_step, 0)

    def widen_step(j, carry):
        wide[pl.ds(j * 256, 256), :] = landed[pl.ds(j * 8, 8)].reshape(256, 128).astype(F32)
        return carry

    lax.fori_loop(0, 8, widen_step, 0)

    def gather_step(t, carry):
        for c in range(2):
            for j in range(5):
                tiles[t, c, :, 128 * j:128 * j + 128] = wide[pl.ds(c * 32 + t * 5 + j, 32, stride=64), :]
        return carry

    lax.fori_loop(0, 6, gather_step, 0)

    def norm_step(t, carry):
        values = tiles[t].reshape(64, 640)
        raw[t] = values[:, 0:384].astype(BF16)
        high, low = squares_split(values)
        meansq = (dot(high, ones) + dot(low, ones)) * (1.0 / 96.0)
        second = normsilu(values, meansq, gain_lanes)
        windows[1, t] = second.astype(BF16)
        spot = iota2((64, 640), 0) % 32
        windows[0, t] = jnp.where(spot == 0, 0.0, pltpu.roll(second, 1, 0)).astype(BF16)
        windows[2, t] = jnp.where(spot == 31, 0.0, pltpu.roll(second, 63, 0)).astype(BF16)
        return carry

    lax.fori_loop(0, 6, norm_step, 0)

    def conv(weights, direct, lane_sets):
        acc = dot(raw[2:6].reshape(256, 384), direct[...])
        for a in range(3):
            for i in range(3):
                window = jnp.concatenate(
                    [windows[i, a:a + 4, :, lo:hi].reshape(256, hi - lo) for lo, hi in lane_sets], 1)
                acc += dot(window, weights[3 * a + i])
        return acc.astype(BF16).reshape(4, 2, 32, 384)

    left = conv(wa, wsa, ((0, 256), (384, 512)))
    for c in range(2):
        out[c, :, :, 0:384] = left[:, c]
    right = conv(wb, wsb, ((512, 640), (128, 384)))
    for c in range(2):
        out[c, :, :, 384:768] = right[:, c]

    def sent_step(step, carry):
        outgoing(step).wait_send()
        return carry

    lax.fori_loop(1, total, sent_step, 0)


def vmem(shape, dtype=BF16):
    return pltpu.VMEM(shape, dtype)


def shards(row_total, tm_total, clip_total, video, gain_first, conv_first, down, gain_second, conv_second, shortcut):
    whole = pl.BlockSpec(memory_space=pltpu.VMEM)
    message = pl.pallas_call(
        functools.partial(section_kernel, row_total, tm_total),
        out_shape=jax.ShapeDtypeStruct((64, 32, 128), BF16),
        in_specs=[whole] * 4,
        out_specs=whole,
        scratch_shapes=[
            vmem((6, 4, 128, 384)),
            vmem((2, 6, 4, 128, 128)),
            vmem((4, 2, 128, 384)),
            vmem((9, 384, 256)),
            vmem((9, 384, 256)),
            vmem((3, 512, 256)),
            vmem((3, 512, 256)),
            vmem((4, 2, 128, 384)),
            vmem((4, 64, 384)),
            vmem((4, 64, 384)),
            vmem((6, 64, 384)),
            vmem((2048, 128), F32),
            pltpu.SemaphoreType.DMA((9,)),
            pltpu.SemaphoreType.DMA((9,)),
        ],
        compiler_params=pltpu.CompilerParams(
            collective_id=0, has_side_effects=True, vmem_limit_bytes=VMEM_LIMIT),
        name="section",
    )(
        video.reshape(4, 2, 128, 384), gain_first.reshape(1, 96),
        conv_first.reshape(9, 288, 96), down.reshape(3, 288, 96),
    )
    latents = pl.pallas_call(
        functools.partial(latent_kernel, row_total, clip_total),
        out_shape=jax.ShapeDtypeStruct((2, 4, 32, 768), BF16),
        in_specs=[whole] * 4,
        out_specs=whole,
        scratch_shapes=[
            vmem((64, 32, 128)),
            vmem((2048, 128), F32),
            vmem((6, 2, 32, 640), F32),
            vmem((3, 6, 64, 640)),
            vmem((6, 64, 384)),
            vmem((9, 384, 384)),
            vmem((9, 384, 384)),
            vmem((384, 384)),
            vmem((384, 384)),
            pltpu.SemaphoreType.DMA((64,)),
            pltpu.SemaphoreType.DMA((64,)),
            pltpu.SemaphoreType.DMA,
        ],
        compiler_params=pltpu.CompilerParams(
            collective_id=1, has_side_effects=True, vmem_limit_bytes=VMEM_LIMIT),
        name="latent",
    )(
        message, gain_second.reshape(1, 96),
        conv_second.reshape(9, 288, 192), shortcut,
    )
    return latents.reshape(2, 4, 32, 1, 768)


def solution(mesh):
    return jax.shard_map(
        functools.partial(shards, mesh.shape["rows"], mesh.shape["tm"], mesh.shape["clip"]),
        mesh=mesh,
        in_specs=(P("clip", "tm", "rows", None, None), P(), P(), P(), P(), P(), P()),
        out_specs=P(None, "tm", None, ("rows", "clip"), None),
        check_vma=False,
    )
```

```python
import functools

import jax
import jax.numpy as jnp
from jax import lax
from jax.experimental import pallas as pl
from jax.experimental.pallas import tpu as pltpu
from jax.sharding import PartitionSpec as P

MESH = pl.DeviceIdType.MESH
F32 = jnp.float32
BF16 = jnp.bfloat16
VMEM_LIMIT = 56 * 1024 * 1024


def iota2(shape, dim):
    return lax.broadcasted_iota(jnp.int32, shape, dim)


def selector(rows, cols, offset):
    return jnp.where(iota2((rows, cols), 1) == iota2((rows, cols), 0) + offset, 1.0, 0.0).astype(BF16)


def dot(a, b):
    return jnp.dot(a, b, preferred_element_type=F32)


def place_exact(vector, chosen):
    wide = jnp.broadcast_to(vector, (8, vector.shape[1]))
    high = wide.astype(BF16)
    rest = wide - high.astype(F32)
    middle = rest.astype(BF16)
    low = (rest - middle.astype(F32)).astype(BF16)
    return (dot(high, chosen) + dot(middle, chosen) + dot(low, chosen))[0:1]


def squares_split(values):
    square = values * values
    high = square.astype(BF16)
    low = (square - high.astype(F32)).astype(BF16)
    return jnp.concatenate([high, low], 1)


def normsilu(values, meansq, half_gain):
    half = values * lax.rsqrt(meansq + 1e-6) * half_gain
    return half + half * jnp.tanh(half)


def shift_down(x):
    moved = pltpu.roll(x, 1, 0)
    return jnp.where(iota2(x.shape, 0) == 0, 0.0, moved)


def shift_up(x):
    rows = x.shape[0]
    moved = pltpu.roll(x, rows - 1, 0)
    return jnp.where(iota2(x.shape, 0) == rows - 1, 0.0, moved)


def merge(a, b):
    return jnp.concatenate([a[:, 0:128], a[:, 128:256] + b[:, 0:128], b[:, 128:256]], 1)


def group_of(lane):
    left = jnp.where(lane < 416, 2, 4)
    right = jnp.where(lane < 608, 5, 1)
    return jnp.where(lane < 384, lane // 96, jnp.where(lane < 512, left, right))


def channel_of(lane):
    left = jnp.where(lane < 416, lane - 384 + 64, lane - 416)
    right = jnp.where(lane < 608, lane - 512, lane - 608)
    return jnp.where(lane < 384, lane % 96, jnp.where(lane < 512, left, right))


def encoder_kernel(
    sizes,
    video_hbm, gain1_hbm, w1_hbm, wd_hbm, gain2_hbm, w2_hbm, shortcut_hbm,
    out,
    video, gain1, w1, wd, gain2, w2, shortcut,
    ones1, ones2, gain_lanes2,
    first, sides, resid, wa, wb, wda, wdb, acc_a, acc_b, section, part_out, part_in,
    z_out, z_in, yc_wide, yc_out, yc_in,
    tiles, windows, raw, wa2, wb2, wsa, wsb,
    near_send, near_recv, z_send, z_recv, yc_send, yc_recv, load,
):
    row_total, tm_total, clip_total, z_total = sizes
    y_total = row_total // z_total
    square = y_total * clip_total
    tm = lax.axis_index("tm")
    row = lax.axis_index("rows")
    clip = lax.axis_index("clip")
    z, y = row // y_total, row % y_total
    spot = y * clip_total + clip
    has_up, has_down = row > 0, row < row_total - 1
    has_past, has_next = tm > 0, tm < tm_total - 1
    up, down = (tm, row - 1, clip), (tm, row + 1, clip)
    past, after = (tm - 1, row, clip), (tm + 1, row, clip)

    def z_partner(step):
        other = (z + step) % z_total
        return other, (tm, other * y_total + y, clip)

    def square_partner(step):
        other = (spot + step) % square
        return other, (tm, z * y_total + other // clip_total, other % clip_total)

    barrier = pltpu.get_barrier_semaphore()
    for exists, who in ((has_up, up), (has_down, down), (has_past, past), (has_next, after)):
        @pl.when(exists)
        def _():
            pl.semaphore_signal(barrier, inc=1, device_id=who, device_id_type=MESH)
    for step in range(1, z_total):
        pl.semaphore_signal(barrier, inc=1, device_id=z_partner(step)[1], device_id_type=MESH)
    for step in range(1, square):
        pl.semaphore_signal(barrier, inc=1, device_id=square_partner(step)[1], device_id_type=MESH)

    loads = [
        pltpu.make_async_copy(src, dst, load.at[n])
        for n, (src, dst) in enumerate((
            (video_hbm, video), (gain1_hbm, gain1), (w1_hbm, w1), (wd_hbm, wd),
            (gain2_hbm, gain2), (w2_hbm, w2), (shortcut_hbm, shortcut)))]
    for one in loads:
        one.start()

    def remote(src, dst, index, who):
        return pltpu.make_async_remote_copy(
            src_ref=src, dst_ref=dst, send_sem=near_send.at[index], recv_sem=near_recv.at[index],
            device_id=who, device_id_type=MESH)

    ones1[...] = jnp.where(
        iota2((768, 384), 0) % 384 // 96 == iota2((768, 384), 1) // 96, 1.0, 0.0).astype(BF16)
    line = iota2((128, 128), 0)
    order = jnp.where(
        iota2((128, 128), 1) == jnp.where(line < 64, 2 * line, 2 * line - 127), 1.0, 0.0).astype(BF16)
    loads[1].wait()
    gain_lanes1 = 0.5 * place_exact(
        gain1[...], jnp.where(iota2((96, 384), 1) % 96 == iota2((96, 384), 0), 1.0, 0.0).astype(BF16))
    loads[0].wait()

    def norm_first(t):
        values = jnp.concatenate([dot(order, video[t, 0]), dot(order, video[t, 1])], 0)
        resid[t] = values.astype(BF16).reshape(2, 128, 384)
        meansq = dot(squares_split(values), ones1[...]) * (1.0 / 96.0)
        first[t + 2, 1:3] = normsilu(values, meansq, gain_lanes1).astype(BF16).reshape(2, 128, 384)

    norm_first(2)
    norm_first(3)

    count = has_up.astype(jnp.int32) + has_down.astype(jnp.int32) + has_past.astype(jnp.int32) + has_next.astype(jnp.int32)
    pl.semaphore_wait(barrier, count + (z_total - 1) + (square - 1))

    down_late = remote(first.at[4:6, 2], first.at[4:6, 0], 0, down)
    down_early = remote(first.at[2:4, 2], first.at[2:4, 0], 1, down)
    up_late = remote(first.at[4:6, 1], first.at[4:6, 3], 2, up)
    up_early = remote(first.at[2:4, 1], first.at[2:4, 3], 3, up)
    frames = remote(first.at[4:6, 1:3], first.at[0:2, 1:3], 4, after)
    corner_top = remote(first.at[4:6, 0], first.at[0:2, 0], 5, after)
    corner_low = remote(first.at[4:6, 3], first.at[0:2, 3], 6, after)
    partials = [remote(part_out.at[n], part_in.at[n], 7 + n, up) for n in range(2)]
    later = remote(windows.at[1, 4:6], windows.at[1, 0:2], 9, after)

    def when(condition, *steps):
        @pl.when(condition)
        def _():
            for step in steps:
                step()

    when(has_down, down_late.start)
    when(has_up, up_late.start)
    when(has_next, frames.start)
    norm_first(0)
    norm_first(1)
    when(has_down, down_early.start)
    when(has_up, up_early.start)

    @pl.when(jnp.logical_not(has_up))
    def _():
        first[:, 0] = jnp.zeros((6, 128, 384), BF16)

    @pl.when(jnp.logical_not(has_down))
    def _():
        first[:, 3] = jnp.zeros((6, 128, 384), BF16)
        part_in[...] = jnp.zeros((2, 2, 64, 384), BF16)

    @pl.when(jnp.logical_not(has_past))
    def _():
        first[0:2, 1:3] = jnp.zeros((2, 2, 128, 384), BF16)
        windows[1, 0:2] = jnp.zeros((2, 64, 640), BF16)

        @pl.when(has_up)
        def _():
            first[0:2, 0] = jnp.zeros((2, 128, 384), BF16)

        @pl.when(has_down)
        def _():
            first[0:2, 3] = jnp.zeros((2, 128, 384), BF16)

    lane = iota2((96, 1024), 1)
    offset = jnp.where(lane < 256, 0, jnp.where(lane < 512, 256 + 96, jnp.where(lane < 768, 512 + 64, 768 + 160)))
    places = jnp.where(lane == iota2((96, 1024), 0) + offset, 1.0, 0.0).astype(BF16)
    loads[2].wait()

    def weight_step(tap, carry):
        placed = dot(w1[tap], places)
        a0, a1 = placed[:, 0:256], placed[:, 256:512]
        b0, b1 = placed[:, 512:768], placed[:, 768:1024]
        spot = 3 * (tap % 3) + tap // 3
        wa[spot, 0:96] = (a0[96:192] + a1[0:96]).astype(BF16)
        wa[spot, 96:192] = (a0[192:288] + a1[96:192]).astype(BF16)
        wa[spot, 192:288] = a1[192:288].astype(BF16)
        wa[spot, 288:384] = a0[0:96].astype(BF16)
        wb[spot, 0:96] = b1[192:288].astype(BF16)
        wb[spot, 96:192] = b0[0:96].astype(BF16)
        wb[spot, 192:288] = (b0[96:192] + b1[0:96]).astype(BF16)
        wb[spot, 288:384] = (b0[192:288] + b1[96:192]).astype(BF16)
        return carry

    lax.fori_loop(0, 9, weight_step, 0)

    lane64 = iota2((64, 128), 1)

    def side_tiles(t, r):
        e0 = first[t, r, 0:64, 0:128].astype(F32)
        o0 = first[t, r, 64:128, 0:128].astype(F32)
        e2 = first[t, r, 0:64, 256:384].astype(F32)
        o2 = first[t, r, 64:128, 256:384].astype(F32)
        sides[0, t, r, 0:64] = jnp.where(lane64 < 32, e2, shift_down(o2)).astype(BF16)
        sides[0, t, r, 64:128] = jnp.where(lane64 < 32, o2, e2).astype(BF16)
        sides[1, t, r, 0:64] = jnp.where(lane64 < 96, o0, e0).astype(BF16)
        sides[1, t, r, 64:128] = jnp.where(lane64 < 96, shift_up(e0), o0).astype(BF16)

    def conv_part(r, taps, t):
        left, right = [], []
        for i in taps:
            for a in range(3):
                cells = slice(t + a, t + a + 2)
                left += [
                    first[cells, r + i, :, 0:256].reshape(256, 256),
                    sides[0, cells, r + i].reshape(256, 128)]
                right += [
                    sides[1, cells, r + i].reshape(256, 128),
                    first[cells, r + i, :, 128:384].reshape(256, 256)]
        lo, hi = 3 * taps[0], 3 * taps[-1] + 3
        deep = (hi - lo) * 384
        return (dot(jnp.concatenate(left, 1), wa[lo:hi].reshape(deep, 256)),
                dot(jnp.concatenate(right, 1), wb[lo:hi].reshape(deep, 256)))

    def conv_local(t):
        for r, taps in ((0, (1, 2)), (1, (0, 1))):
            part_a, part_b = conv_part(r, taps, t)
            acc_a[r, t:t + 2] = part_a.reshape(2, 128, 256)
            acc_b[r, t:t + 2] = part_b.reshape(2, 128, 256)

    def conv_finish(r, t):
        part_a, part_b = conv_part(r, (0,) if r == 0 else (2,), t)
        part_a += acc_a[r, t:t + 2].reshape(256, 256)
        part_b += acc_b[r, t:t + 2].reshape(256, 256)
        total = merge(part_a, part_b) + resid[t:t + 2, r].reshape(256, 384).astype(F32)
        section[t:t + 2, r] = total.astype(BF16).reshape(2, 128, 384)

    for t in (4, 5, 2, 3):
        for r in (1, 2):
            side_tiles(t, r)
    conv_local(2)

    def forward_top():
        down_late.wait_recv()
        when(has_next, corner_top.start)

    def forward_low():
        up_late.wait_recv()
        when(has_next, corner_low.start)

    when(has_up, forward_top)
    when(has_down, forward_low)

    loads[3].wait()

    def down_weight_step(tap, carry):
        placed = dot(wd[tap], places)
        for ref, base in ((wda, 0), (wdb, 512)):
            p0, p1 = placed[:, base:base + 256], placed[:, base + 256:base + 512]
            ref[tap, 0:96] = p0[0:96].astype(BF16)
            ref[tap, 96:192] = p0[96:192].astype(BF16)
            ref[tap, 192:288] = (p0[192:288] + p1[0:96]).astype(BF16)
            ref[tap, 288:384] = p1[96:192].astype(BF16)
            ref[tap, 384:480] = p1[192:288].astype(BF16)
            ref[tap, 480:512] = jnp.zeros((32, 256), BF16)
        return carry

    lax.fori_loop(0, 3, down_weight_step, 0)

    lane2 = iota2((192, 768), 1)
    source2 = iota2((192, 768), 0)
    places2 = jnp.where(lane2 == jnp.where(lane2 < 384, source2, source2 + 576), 1.0, 0.0).astype(BF16)
    loads[5].wait()

    def weight2_step(tap, carry):
        placed = dot(w2[tap], places2)
        p0, p1 = placed[:, 0:384], placed[:, 384:768]
        wa2[tap, 0:96] = (p0[96:192] + p1[0:96]).astype(BF16)
        wa2[tap, 96:192] = (p0[192:288] + p1[96:192]).astype(BF16)
        wa2[tap, 192:288] = p1[192:288].astype(BF16)
        wa2[tap, 288:384] = p0[0:96].astype(BF16)
        wb2[tap, 0:96] = p1[192:288].astype(BF16)
        wb2[tap, 96:192] = p0[0:96].astype(BF16)
        wb2[tap, 192:288] = (p0[96:192] + p1[0:96]).astype(BF16)
        wb2[tap, 288:384] = (p0[192:288] + p1[96:192]).astype(BF16)
        return carry

    lax.fori_loop(0, 9, weight2_step, 0)

    def halo_frames():
        frames.wait_recv()

    when(has_past, halo_frames)
    for t in (0, 1):
        for r in (1, 2):
            side_tiles(t, r)
    conv_local(0)

    loads[6].wait()
    placed2 = dot(shortcut[...], places2).astype(BF16)
    wsa[0:96] = placed2[:, 0:384]
    wsa[96:192] = placed2[:, 384:768]
    wsa[192:384] = jnp.zeros((192, 384), BF16)
    wsb[0:192] = jnp.zeros((192, 384), BF16)
    wsb[192:288] = placed2[:, 0:384]
    wsb[288:384] = placed2[:, 384:768]
    rows640 = iota2((640, 640), 0)
    twice = jnp.logical_or(jnp.logical_and(rows640 >= 384, rows640 < 416), rows640 >= 608)
    from_group = jnp.where(twice, -1, group_of(rows640))
    same = jnp.where(from_group == group_of(iota2((640, 640), 1)), 1.0, 0.0).astype(BF16)
    ones2[0:640] = same
    ones2[640:1280] = same
    loads[4].wait()
    gain_lanes2[...] = jnp.broadcast_to(0.5 * place_exact(gain2[...], jnp.where(
        channel_of(iota2((96, 640), 1)) == iota2((96, 640), 0), 1.0, 0.0).astype(BF16)), (8, 640))

    def down_rows(t, r):
        pieces = [], []
        for f in (t, t + 1):
            even = section[f, r, 0:64]
            odd = section[f, r, 64:128]
            following = shift_up(even[:, 0:128].astype(F32)).astype(BF16)
            pieces[0].append(jnp.concatenate([even, odd[:, 0:128]], 1))
            pieces[1].append(jnp.concatenate([odd, following], 1))
        return jnp.concatenate(pieces[0], 0), jnp.concatenate(pieces[1], 0)

    when(has_up, down_early.wait_recv)
    for half, t in ((0, 2), (1, 0)):
        if half == 0:
            frames_here = (4, 5, 2, 3)
        else:
            frames_here = (0, 1)

            @pl.when(jnp.logical_and(has_past, has_up))
            def _():
                corner_top.wait_recv()
        for f in frames_here:
            side_tiles(f, 0)
        conv_finish(0, t)
        left, right = down_rows(t, 0)
        part_out[half] = merge(dot(left, wda[2]), dot(right, wdb[2])).astype(BF16).reshape(2, 64, 384)
        when(has_up, partials[half].start)

    when(has_down, up_early.wait_recv)
    for f in (4, 5, 2, 3):
        side_tiles(f, 3)
    conv_finish(1, 2)

    def reduce_half(half, t):
        left0, right0 = down_rows(t, 0)
        left1, right1 = down_rows(t, 1)
        own = merge(dot(left0, wda[0]) + dot(left1, wda[1]), dot(right0, wdb[0]) + dot(right1, wdb[1]))
        when(has_down, partials[half].wait_recv)
        total = (own + part_in[half].reshape(128, 384).astype(F32)).astype(BF16).astype(F32)
        spot_in_block = iota2((64, 128), 0) % 8
        wide = []
        for f in range(2):
            cell = total[64 * f:64 * f + 64]
            edge = jnp.where(spot_in_block < 4, shift_down(cell[:, 256:384]), shift_up(cell[:, 0:128]))
            wide.append(jnp.concatenate([cell, edge], 1).reshape(z_total, 8, 512))
        z_out[half] = jnp.concatenate(wide, 1).astype(BF16)

    def z_copy(half, step, arriving):
        other, who = z_partner(step)
        here = (z - step + z_total) % z_total
        slot = half * z_total + step
        return pltpu.make_async_remote_copy(
            src_ref=z_out.at[half, other], dst_ref=z_in.at[half, here if arriving else z],
            send_sem=z_send.at[slot], recv_sem=z_recv.at[slot], device_id=who, device_id_type=MESH)

    def send_z(half):
        for step in range(1, z_total):
            z_copy(half, step, False).start()
        z_in[half, z] = z_out[half, z]

    reduce_half(0, 2)
    send_z(0)

    @pl.when(jnp.logical_and(has_past, has_down))
    def _():
        corner_low.wait_recv()
    for f in (0, 1):
        side_tiles(f, 3)
    conv_finish(1, 0)
    reduce_half(1, 0)
    send_z(1)

    def yc_copy(half, step, arriving):
        other, who = square_partner(step)
        here = (spot - step + square) % square
        slot = half * square + step
        return pltpu.make_async_remote_copy(
            src_ref=yc_out.at[half, other], dst_ref=yc_in.at[half, here if arriving else spot],
            send_sem=yc_send.at[slot], recv_sem=yc_recv.at[slot], device_id=who, device_id_type=MESH)

    lane8 = iota2((8, 128), 1)
    line8 = iota2((8, 128), 0)

    def relay(half):
        for step in range(1, z_total):
            z_copy(half, step, True).wait_recv()
        for source in range(z_total):
            cells = z_in[half, source].astype(F32)
            for f in range(2):
                cell = cells[8 * f:8 * f + 8]
                t0, t1, t2, edge = (cell[:, 128 * n:128 * n + 128] for n in range(4))
                before = jnp.where(line8 == 0, edge, pltpu.roll(t2, 1, 0))
                following = jnp.where(line8 == 7, edge, pltpu.roll(t0, 7, 0))
                parts = (t0, t1, t2, jnp.where(lane8 < 32, t2, before), jnp.where(lane8 < 96, following, t0))
                for n, part in enumerate(parts):
                    yc_wide[n, pl.ds(f * 8 + source, 8, stride=16), :] = part
        for n in range(5):
            yc_out[half, :, :, 128 * n:128 * n + 128] = yc_wide[n].astype(BF16).reshape(8, 16, 128)
        for step in range(1, square):
            yc_copy(half, step, False).start()
        yc_in[half, spot] = yc_out[half, spot]

    relay(0)
    relay(1)

    def norm_second(half, t):
        for step in range(1, square):
            yc_copy(half, step, True).wait_recv()
        for source in range(square):
            cells = yc_in[half, source].astype(F32)
            start = (source % clip_total) * row_total + source // clip_total
            for f in range(2):
                for n in range(5):
                    tiles[n, pl.ds(64 * f + start, 8, stride=y_total), :] = cells[8 * f:8 * f + 8, 128 * n:128 * n + 128]
        values = jnp.concatenate([tiles[n] for n in range(5)], 1)
        raw[t:t + 2] = values[:, 0:384].astype(BF16).reshape(2, 64, 384)
        meansq = dot(squares_split(values), ones2[...]) * (1.0 / 96.0)
        second = normsilu(values, meansq, gain_lanes2[0:1])
        windows[1, t + 2:t + 4] = second.astype(BF16).reshape(2, 64, 640)
        return second

    def shifted(second, t):
        line = iota2((128, 640), 0) % 32
        windows[0, t:t + 2] = jnp.where(line == 0, 0.0, pltpu.roll(second, 1, 0)).astype(BF16).reshape(2, 64, 640)
        windows[2, t:t + 2] = jnp.where(line == 31, 0.0, pltpu.roll(second, 127, 0)).astype(BF16).reshape(2, 64, 640)

    second = norm_second(0, 2)
    when(has_next, later.start)
    shifted(second, 4)
    second = norm_second(1, 0)
    shifted(second, 2)
    when(has_past, later.wait_recv)
    shifted(windows[1, 0:2].reshape(128, 640).astype(F32), 0)

    def conv(weights, direct, lane_sets):
        acc = dot(raw[...].reshape(256, 384), direct[...])
        for a in range(3):
            pieces = []
            for i in range(3):
                pieces += [windows[i, a:a + 4, :, lo:hi].reshape(256, hi - lo) for lo, hi in lane_sets]
            acc += dot(jnp.concatenate(pieces, 1), weights[3 * a:3 * a + 3].reshape(1152, 384))
        return acc.astype(BF16).reshape(4, 2, 32, 384)

    left = conv(wa2, wsa, ((0, 256), (384, 512)))
    for c in range(2):
        out[c, :, :, 0:384] = left[:, c]
    right = conv(wb2, wsb, ((512, 640), (128, 384)))
    for c in range(2):
        out[c, :, :, 384:768] = right[:, c]

    when(has_down, down_late.wait_send, down_early.wait_send)
    when(has_up, up_late.wait_send, up_early.wait_send, partials[0].wait_send, partials[1].wait_send)
    when(has_next, frames.wait_send, later.wait_send)

    @pl.when(jnp.logical_and(has_next, has_up))
    def _():
        corner_top.wait_send()

    @pl.when(jnp.logical_and(has_next, has_down))
    def _():
        corner_low.wait_send()

    for half in range(2):
        for step in range(1, z_total):
            z_copy(half, step, False).wait_send()
        for step in range(1, square):
            yc_copy(half, step, False).wait_send()


def vmem(shape, dtype=BF16):
    return pltpu.VMEM(shape, dtype)


def shards(sizes, video, gain_first, conv_first, down, gain_second, conv_second, shortcut):
    dma = pltpu.SemaphoreType.DMA
    latents = pl.pallas_call(
        functools.partial(encoder_kernel, sizes),
        out_shape=jax.ShapeDtypeStruct((2, 4, 32, 768), BF16),
        in_specs=[pl.BlockSpec(memory_space=pl.ANY)] * 7,
        out_specs=pl.BlockSpec(memory_space=pltpu.VMEM),
        scratch_shapes=[
            vmem((4, 2, 128, 384)), vmem((1, 96), F32), vmem((9, 288, 96)), vmem((3, 288, 96)),
            vmem((1, 96), F32), vmem((9, 288, 192)), vmem((96, 192)),
            vmem((768, 384)), vmem((1280, 640)), vmem((8, 640), F32),
            vmem((6, 4, 128, 384)), vmem((2, 6, 4, 128, 128)), vmem((4, 2, 128, 384)),
            vmem((9, 384, 256)), vmem((9, 384, 256)), vmem((3, 512, 256)), vmem((3, 512, 256)),
            vmem((2, 4, 128, 256), F32), vmem((2, 4, 128, 256), F32),
            vmem((4, 2, 128, 384)),
            vmem((2, 2, 64, 384)), vmem((2, 2, 64, 384)),
            vmem((2, 8, 16, 512)), vmem((2, 8, 16, 512)),
            vmem((5, 128, 128), F32), vmem((2, 8, 16, 640)), vmem((2, 8, 16, 640)),
            vmem((5, 128, 128), F32), vmem((3, 6, 64, 640)), vmem((4, 64, 384)),
            vmem((9, 384, 384)), vmem((9, 384, 384)), vmem((384, 384)), vmem((384, 384)),
            dma((10,)), dma((10,)), dma((16,)), dma((16,)), dma((16,)), dma((16,)), dma((7,)),
        ],
        compiler_params=pltpu.CompilerParams(
            collective_id=0, has_side_effects=True, vmem_limit_bytes=VMEM_LIMIT),
        name="encoder",
    )(
        video.reshape(4, 2, 128, 384), gain_first.reshape(1, 96),
        conv_first.reshape(9, 288, 96), down.reshape(3, 288, 96),
        gain_second.reshape(1, 96), conv_second.reshape(9, 288, 192), shortcut,
    )
    return latents.reshape(2, 4, 32, 1, 768)


def solution(mesh):
    sizes = (mesh.shape["rows"], mesh.shape["tm"], mesh.shape["clip"], 8)
    return jax.shard_map(
        functools.partial(shards, sizes),
        mesh=mesh,
        in_specs=(P("clip", "tm", "rows", None, None), P(), P(), P(), P(), P(), P()),
        out_specs=P(None, "tm", None, ("rows", "clip"), None),
        check_vma=False,
    )
```

```python
import functools

import jax
import jax.numpy as jnp
from jax import lax
from jax.experimental import pallas as pl
from jax.experimental.pallas import tpu as pltpu
from jax.sharding import PartitionSpec as P

MESH = pl.DeviceIdType.MESH
F32 = jnp.float32
BF16 = jnp.bfloat16
VMEM_LIMIT = 56 * 1024 * 1024


def iota2(shape, dim):
    return lax.broadcasted_iota(jnp.int32, shape, dim)


def selector(rows, cols, offset):
    return jnp.where(iota2((rows, cols), 1) == iota2((rows, cols), 0) + offset, 1.0, 0.0).astype(BF16)


def dot(a, b):
    return jnp.dot(a, b, preferred_element_type=F32)


def place_exact(vector, chosen):
    wide = jnp.broadcast_to(vector, (8, vector.shape[1]))
    high = wide.astype(BF16)
    rest = wide - high.astype(F32)
    middle = rest.astype(BF16)
    low = (rest - middle.astype(F32)).astype(BF16)
    return (dot(high, chosen) + dot(middle, chosen) + dot(low, chosen))[0:1]


def squares_split(values):
    square = values * values
    high = square.astype(BF16)
    low = (square - high.astype(F32)).astype(BF16)
    return jnp.concatenate([high, low], 1)


def normsilu(values, meansq, half_gain):
    half = values * lax.rsqrt(meansq + 1e-6) * half_gain
    return half + half * jnp.tanh(half)


def shift_down(x):
    moved = pltpu.roll(x, 1, 0)
    return jnp.where(iota2(x.shape, 0) == 0, 0.0, moved)


def shift_up(x):
    rows = x.shape[0]
    moved = pltpu.roll(x, rows - 1, 0)
    return jnp.where(iota2(x.shape, 0) == rows - 1, 0.0, moved)


def packed(cells):
    c0, c1, c2, c3 = cells
    lane = iota2(c0.shape, 1)
    c1, c2, c3 = pltpu.roll(c1, 96, 1), pltpu.roll(c2, 64, 1), pltpu.roll(c3, 32, 1)
    return jnp.concatenate(
        [jnp.where(lane < 96, c0, c1), jnp.where(lane < 64, c1, c2), jnp.where(lane < 32, c2, c3)], 1)


def group_of(lane):
    left = jnp.where(lane < 416, 2, 4)
    right = jnp.where(lane < 608, 5, 1)
    return jnp.where(lane < 384, lane // 96, jnp.where(lane < 512, left, right))


def channel_of(lane):
    left = jnp.where(lane < 416, lane - 384 + 64, lane - 416)
    right = jnp.where(lane < 608, lane - 512, lane - 608)
    return jnp.where(lane < 384, lane % 96, jnp.where(lane < 512, left, right))


def encoder_kernel(
    sizes,
    video_hbm, gain1_hbm, w1_hbm, wd_hbm, gain2_hbm, w2_hbm, shortcut_hbm,
    out,
    video, gain1, w1, wd, gain2, w2, shortcut,
    ones1, ones2, gain_lanes2,
    first, cells1, cellsv, wdp, products, w5, part_out, part_in, own_sum,
    z_out, z_in, yc_wide, yc_out, yc_in,
    tiles, windows, raw, wa2, wb2, wsa, wsb,
    near_send, near_recv, z_send, z_recv, yc_send, yc_recv, load,
):
    row_total, tm_total, clip_total, z_total = sizes
    y_total = row_total // z_total
    square = y_total * clip_total
    tm = lax.axis_index("tm")
    row = lax.axis_index("rows")
    clip = lax.axis_index("clip")
    z, y = row // y_total, row % y_total
    spot = y * clip_total + clip
    has_up, has_down = row > 0, row < row_total - 1
    has_past, has_next = tm > 0, tm < tm_total - 1
    up, down = (tm, row - 1, clip), (tm, row + 1, clip)
    past, after = (tm - 1, row, clip), (tm + 1, row, clip)

    def z_partner(step):
        other = (z + step) % z_total
        return other, (tm, other * y_total + y, clip)

    def square_partner(step):
        other = (spot + step) % square
        return other, (tm, z * y_total + other // clip_total, other % clip_total)

    barrier = pltpu.get_barrier_semaphore()
    for exists, who in ((has_up, up), (has_down, down), (has_past, past), (has_next, after)):
        @pl.when(exists)
        def _():
            pl.semaphore_signal(barrier, inc=1, device_id=who, device_id_type=MESH)
    for step in range(1, z_total):
        pl.semaphore_signal(barrier, inc=1, device_id=z_partner(step)[1], device_id_type=MESH)
    for step in range(1, square):
        pl.semaphore_signal(barrier, inc=1, device_id=square_partner(step)[1], device_id_type=MESH)

    loads = [
        pltpu.make_async_copy(src, dst, load.at[n])
        for n, (src, dst) in enumerate((
            (video_hbm, video), (gain1_hbm, gain1), (w1_hbm, w1), (wd_hbm, wd),
            (gain2_hbm, gain2), (w2_hbm, w2), (shortcut_hbm, shortcut)))]
    for one in loads:
        one.start()

    def remote(src, dst, index, who):
        return pltpu.make_async_remote_copy(
            src_ref=src, dst_ref=dst, send_sem=near_send.at[index], recv_sem=near_recv.at[index],
            device_id=who, device_id_type=MESH)

    ones1[...] = jnp.where(
        iota2((768, 384), 0) % 384 // 96 == iota2((768, 384), 1) // 96, 1.0, 0.0).astype(BF16)
    line = iota2((128, 128), 0)
    order = jnp.where(
        iota2((128, 128), 1) == jnp.where(line < 64, 2 * line, 2 * line - 127), 1.0, 0.0).astype(BF16)
    loads[1].wait()
    gain_lanes1 = 0.5 * place_exact(
        gain1[...], jnp.where(iota2((96, 384), 1) % 96 == iota2((96, 384), 0), 1.0, 0.0).astype(BF16))
    loads[0].wait()

    lane64 = iota2((64, 128), 1)
    line64 = iota2((64, 128), 0)

    def windows_of(even, odd):
        return shift_up(even[:, 0:128]), shift_up(even[:, 128:256]), shift_down(odd[:, 256:384])

    def spread_first(t, r, even, odd):
        after0, after1, before2 = windows_of(even, odd)
        last = jnp.where(line64 == 63, pltpu.roll(odd[:, 256:384], 32, 1), 0.0)
        cells1[t, r, 0] = jnp.concatenate([
            even, odd[:, 0:128], jnp.where(lane64 < 64, odd[:, 128:256], 0.0),
            jnp.where(lane64 < 32, 0.0, before2)], 1).astype(BF16)
        cells1[t, r, 1] = jnp.concatenate([
            odd, after0, jnp.where(lane64 < 64, after1, last),
            jnp.where(lane64 < 32, last, even[:, 256:384])], 1).astype(BF16)

    def norm_first(t):
        values = jnp.concatenate([dot(order, video[t, 0]), dot(order, video[t, 1])], 0)
        meansq = dot(squares_split(values), ones1[...]) * (1.0 / 96.0)
        result = normsilu(values, meansq, gain_lanes1)
        first[t + 2] = result.astype(BF16).reshape(2, 128, 384)
        for r in range(2):
            even, odd = values[128 * r:128 * r + 64], values[128 * r + 64:128 * r + 128]
            cellsv[t, r, 0] = jnp.concatenate([even, odd[:, 0:128]], 1).astype(BF16)
            cellsv[t, r, 1] = jnp.concatenate([odd, shift_up(even[:, 0:128])], 1).astype(BF16)
            even, odd = result[128 * r:128 * r + 64], result[128 * r + 64:128 * r + 128]
            spread_first(t + 2, r, even, odd)

    norm_first(2)
    norm_first(3)

    count = has_up.astype(jnp.int32) + has_down.astype(jnp.int32) + has_past.astype(jnp.int32) + has_next.astype(jnp.int32)
    pl.semaphore_wait(barrier, count + (z_total - 1) + (square - 1))

    frames = remote(first.at[4:6], first.at[0:2], 0, after)
    ups = [remote(part_out.at[0, n], part_in.at[0, n], 1 + n, up) for n in range(2)]
    downs = [remote(part_out.at[1, n], part_in.at[1, n], 3 + n, down) for n in range(2)]
    later = remote(windows.at[1, 4:6], windows.at[1, 0:2], 5, after)

    def when(condition, *steps):
        @pl.when(condition)
        def _():
            for step in steps:
                step()

    when(has_next, frames.start)
    norm_first(0)
    norm_first(1)

    @pl.when(jnp.logical_not(has_up))
    def _():
        part_in[1] = jnp.zeros((2, 128, 384), BF16)

    @pl.when(jnp.logical_not(has_down))
    def _():
        part_in[0] = jnp.zeros((2, 128, 384), BF16)

    @pl.when(jnp.logical_not(has_past))
    def _():
        first[0:2] = jnp.zeros((2, 2, 128, 384), BF16)
        windows[1, 0:2] = jnp.zeros((2, 64, 640), BF16)

    loads[3].wait()
    wdp[...] = jnp.zeros((96, 1152), BF16)
    for i in range(3):
        for j in range(3):
            wdp[:, 128 * (3 * i + j):128 * (3 * i + j) + 96] = wd[i, 96 * j:96 * j + 96]
    blank = jnp.zeros((96, 128), F32)

    def down_tap(i, j):
        return wdp[:, 128 * (3 * i + j):128 * (3 * i + j) + 128]

    for r, i in ((1, 0), (2, 1), (3, 2)):
        none = blank.astype(BF16)
        for n, (q0, q1) in enumerate((
                (down_tap(i, 0), none), (down_tap(i, 1), none), (down_tap(i, 2), down_tap(i, 0)),
                (none, down_tap(i, 1)), (none, down_tap(i, 2)))):
            w5[r, 2304 + 96 * n:2400 + 96 * n] = jnp.concatenate([q0, q1], 1)
        w5[r, 2784:2816] = jnp.zeros((32, 256), BF16)
    below = has_down.astype(F32)
    loads[2].wait()

    def compose_step(a, carry):
        for i in range(3):
            products[i] = dot(w1[3 * a + i], wdp[...])

        def total(r, pairs):
            result = None
            for i in range(3):
                lower = r - i
                if 0 <= lower <= 2:
                    for j, across in pairs:
                        lane = 128 * (3 * lower + across)
                        term = products[i, 96 * j:96 * j + 96, lane:lane + 128]
                        if r == 2 and lower == 2:
                            term = term * below
                        result = term if result is None else result + term
            return result

        start = pl.multiple_of(a * 768, 128)
        for r in range(5):
            at = [total(r, [(j, c - j) for j in range(3) if 0 <= c - j <= 2]) for c in range(5)]
            beyond = -total(r, [(0, 2)])
            for n, (q0, q1) in enumerate((
                    (at[1], blank), (at[2], at[0]), (at[3], at[1]), (at[4], at[2]),
                    (blank, at[3]), (blank, at[4]), (blank, beyond), (at[0], blank))):
                w5[r, pl.ds(start + 96 * n, 96)] = jnp.concatenate([q0, q1], 1).astype(BF16)
        return carry

    lax.fori_loop(0, 3, compose_step, 0)

    def row_cells(t, r, with_video):
        pieces = [cells1[t + a:t + a + 2, r].reshape(256, 768) for a in range(3)]
        if with_video:
            pieces.append(cellsv[t:t + 2, r].reshape(256, 512))
        return jnp.concatenate(pieces, 1)

    def compact(total):
        frames_here = []
        for f in range(2):
            base = 128 * f
            frames_here.append(packed([
                total[base + 64 * p:base + 64 * p + 64, 128 * q:128 * q + 128]
                for p in range(2) for q in range(2)]))
        return jnp.concatenate(frames_here, 0)

    def send_partials(half, t):
        total = dot(row_cells(t, 0, True), w5[3]) + dot(row_cells(t, 1, False), w5[4, 0:2304])
        part_out[0, half] = compact(total).astype(BF16)
        when(has_up, ups[half].start)
        part_out[1, half] = compact(dot(row_cells(t, 1, False), w5[0, 0:2304])).astype(BF16)
        when(has_down, downs[half].start)

    def sum_own(half, t):
        total = dot(row_cells(t, 0, True), w5[1]) + dot(row_cells(t, 1, True), w5[2])
        own_sum[half] = compact(total)

    send_partials(0, 2)

    def halo_frames():
        frames.wait_recv()

    when(has_past, halo_frames)
    for t in range(2):
        for r in range(2):
            cell = first[t, r].astype(F32)
            spread_first(t, r, cell[0:64], cell[64:128])
    send_partials(1, 0)
    sum_own(0, 2)
    sum_own(1, 0)

    lane2 = iota2((192, 768), 1)
    source2 = iota2((192, 768), 0)
    places2 = jnp.where(lane2 == jnp.where(lane2 < 384, source2, source2 + 576), 1.0, 0.0).astype(BF16)
    loads[5].wait()

    def weight2_step(tap, carry):
        placed = dot(w2[tap], places2)
        p0, p1 = placed[:, 0:384], placed[:, 384:768]
        wa2[tap, 0:96] = (p0[96:192] + p1[0:96]).astype(BF16)
        wa2[tap, 96:192] = (p0[192:288] + p1[96:192]).astype(BF16)
        wa2[tap, 192:288] = p1[192:288].astype(BF16)
        wa2[tap, 288:384] = p0[0:96].astype(BF16)
        wb2[tap, 0:96] = p1[192:288].astype(BF16)
        wb2[tap, 96:192] = p0[0:96].astype(BF16)
        wb2[tap, 192:288] = (p0[96:192] + p1[0:96]).astype(BF16)
        wb2[tap, 288:384] = (p0[192:288] + p1[96:192]).astype(BF16)
        return carry

    lax.fori_loop(0, 9, weight2_step, 0)

    loads[6].wait()
    placed2 = dot(shortcut[...], places2).astype(BF16)
    wsa[0:96] = placed2[:, 0:384]
    wsa[96:192] = placed2[:, 384:768]
    wsa[192:384] = jnp.zeros((192, 384), BF16)
    wsb[0:192] = jnp.zeros((192, 384), BF16)
    wsb[192:288] = placed2[:, 0:384]
    wsb[288:384] = placed2[:, 384:768]
    rows640 = iota2((640, 640), 0)
    twice = jnp.logical_or(jnp.logical_and(rows640 >= 384, rows640 < 416), rows640 >= 608)
    from_group = jnp.where(twice, -1, group_of(rows640))
    same = jnp.where(from_group == group_of(iota2((640, 640), 1)), 1.0, 0.0).astype(BF16)
    ones2[0:640] = same
    ones2[640:1280] = same
    loads[4].wait()
    gain_lanes2[...] = jnp.broadcast_to(0.5 * place_exact(gain2[...], jnp.where(
        channel_of(iota2((96, 640), 1)) == iota2((96, 640), 0), 1.0, 0.0).astype(BF16)), (8, 640))

    def reduce_half(half):
        when(has_down, ups[half].wait_recv)
        when(has_up, downs[half].wait_recv)
        total = own_sum[half] + part_in[0, half].astype(F32) + part_in[1, half].astype(F32)
        total = total.astype(BF16).astype(F32)
        spot_in_block = iota2((64, 128), 0) % 8
        wide = []
        for f in range(2):
            cell = total[64 * f:64 * f + 64]
            edge = jnp.where(spot_in_block < 4, shift_down(cell[:, 256:384]), shift_up(cell[:, 0:128]))
            wide.append(jnp.concatenate([cell, edge], 1).reshape(z_total, 8, 512))
        z_out[half] = jnp.concatenate(wide, 1).astype(BF16)

    def z_copy(half, step, arriving):
        other, who = z_partner(step)
        here = (z - step + z_total) % z_total
        slot = half * z_total + step
        return pltpu.make_async_remote_copy(
            src_ref=z_out.at[half, other], dst_ref=z_in.at[half, here if arriving else z],
            send_sem=z_send.at[slot], recv_sem=z_recv.at[slot], device_id=who, device_id_type=MESH)

    def send_z(half):
        for step in range(1, z_total):
            z_copy(half, step, False).start()
        z_in[half, z] = z_out[half, z]

    reduce_half(0)
    send_z(0)
    reduce_half(1)
    send_z(1)

    def yc_copy(half, step, arriving):
        other, who = square_partner(step)
        here = (spot - step + square) % square
        slot = half * square + step
        return pltpu.make_async_remote_copy(
            src_ref=yc_out.at[half, other], dst_ref=yc_in.at[half, here if arriving else spot],
            send_sem=yc_send.at[slot], recv_sem=yc_recv.at[slot], device_id=who, device_id_type=MESH)

    lane8 = iota2((8, 128), 1)
    line8 = iota2((8, 128), 0)

    def relay(half):
        for step in range(1, z_total):
            z_copy(half, step, True).wait_recv()
        for source in range(z_total):
            cells = z_in[half, source].astype(F32)
            for f in range(2):
                cell = cells[8 * f:8 * f + 8]
                t0, t1, t2, edge = (cell[:, 128 * n:128 * n + 128] for n in range(4))
                before = jnp.where(line8 == 0, edge, pltpu.roll(t2, 1, 0))
                following = jnp.where(line8 == 7, edge, pltpu.roll(t0, 7, 0))
                parts = (t0, t1, t2, jnp.where(lane8 < 32, t2, before), jnp.where(lane8 < 96, following, t0))
                for n, part in enumerate(parts):
                    yc_wide[n, pl.ds(f * 8 + source, 8, stride=16), :] = part
        for n in range(5):
            yc_out[half, :, :, 128 * n:128 * n + 128] = yc_wide[n].astype(BF16).reshape(8, 16, 128)
        for step in range(1, square):
            yc_copy(half, step, False).start()
        yc_in[half, spot] = yc_out[half, spot]

    relay(0)
    relay(1)

    def norm_second(half, t):
        for step in range(1, square):
            yc_copy(half, step, True).wait_recv()
        for source in range(square):
            cells = yc_in[half, source].astype(F32)
            start = (source % clip_total) * row_total + source // clip_total
            for f in range(2):
                for n in range(5):
                    tiles[n, pl.ds(64 * f + start, 8, stride=y_total), :] = cells[8 * f:8 * f + 8, 128 * n:128 * n + 128]
        values = jnp.concatenate([tiles[n] for n in range(5)], 1)
        raw[t:t + 2] = values[:, 0:384].astype(BF16).reshape(2, 64, 384)
        meansq = dot(squares_split(values), ones2[...]) * (1.0 / 96.0)
        second = normsilu(values, meansq, gain_lanes2[0:1])
        windows[1, t + 2:t + 4] = second.astype(BF16).reshape(2, 64, 640)
        return second

    def shifted(second, t):
        line = iota2((128, 640), 0) % 32
        windows[0, t:t + 2] = jnp.where(line == 0, 0.0, pltpu.roll(second, 1, 0)).astype(BF16).reshape(2, 64, 640)
        windows[2, t:t + 2] = jnp.where(line == 31, 0.0, pltpu.roll(second, 127, 0)).astype(BF16).reshape(2, 64, 640)

    second = norm_second(0, 2)
    when(has_next, later.start)
    shifted(second, 4)
    second = norm_second(1, 0)
    shifted(second, 2)
    when(has_past, later.wait_recv)
    shifted(windows[1, 0:2].reshape(128, 640).astype(F32), 0)

    def conv(weights, direct, lane_sets):
        acc = dot(raw[...].reshape(256, 384), direct[...])
        for a in range(3):
            pieces = []
            for i in range(3):
                pieces += [windows[i, a:a + 4, :, lo:hi].reshape(256, hi - lo) for lo, hi in lane_sets]
            acc += dot(jnp.concatenate(pieces, 1), weights[3 * a:3 * a + 3].reshape(1152, 384))
        return acc.astype(BF16).reshape(4, 2, 32, 384)

    left = conv(wa2, wsa, ((0, 256), (384, 512)))
    for c in range(2):
        out[c, :, :, 0:384] = left[:, c]
    right = conv(wb2, wsb, ((512, 640), (128, 384)))
    for c in range(2):
        out[c, :, :, 384:768] = right[:, c]

    when(has_up, ups[0].wait_send, ups[1].wait_send)
    when(has_down, downs[0].wait_send, downs[1].wait_send)
    when(has_next, frames.wait_send, later.wait_send)
    for half in range(2):
        for step in range(1, z_total):
            z_copy(half, step, False).wait_send()
        for step in range(1, square):
            yc_copy(half, step, False).wait_send()


def vmem(shape, dtype=BF16):
    return pltpu.VMEM(shape, dtype)


def shards(sizes, video, gain_first, conv_first, down, gain_second, conv_second, shortcut):
    dma = pltpu.SemaphoreType.DMA
    latents = pl.pallas_call(
        functools.partial(encoder_kernel, sizes),
        out_shape=jax.ShapeDtypeStruct((2, 4, 32, 768), BF16),
        in_specs=[pl.BlockSpec(memory_space=pl.ANY)] * 7,
        out_specs=pl.BlockSpec(memory_space=pltpu.VMEM),
        scratch_shapes=[
            vmem((4, 2, 128, 384)), vmem((1, 96), F32), vmem((9, 288, 96)), vmem((3, 288, 96)),
            vmem((1, 96), F32), vmem((9, 288, 192)), vmem((96, 192)),
            vmem((768, 384)), vmem((1280, 640)), vmem((8, 640), F32),
            vmem((6, 2, 128, 384)), vmem((6, 2, 2, 64, 768)), vmem((4, 2, 2, 64, 512)),
            vmem((96, 1152)), vmem((3, 288, 1152), F32), vmem((5, 2816, 256)),
            vmem((2, 2, 128, 384)), vmem((2, 2, 128, 384)), vmem((2, 128, 384), F32),
            vmem((2, 8, 16, 512)), vmem((2, 8, 16, 512)),
            vmem((5, 128, 128), F32), vmem((2, 8, 16, 640)), vmem((2, 8, 16, 640)),
            vmem((5, 128, 128), F32), vmem((3, 6, 64, 640)), vmem((4, 64, 384)),
            vmem((9, 384, 384)), vmem((9, 384, 384)), vmem((384, 384)), vmem((384, 384)),
            dma((6,)), dma((6,)), dma((16,)), dma((16,)), dma((16,)), dma((16,)), dma((7,)),
        ],
        compiler_params=pltpu.CompilerParams(
            collective_id=0, has_side_effects=True, vmem_limit_bytes=VMEM_LIMIT),
        name="encoder",
    )(
        video.reshape(4, 2, 128, 384), gain_first.reshape(1, 96),
        conv_first.reshape(9, 288, 96), down.reshape(3, 288, 96),
        gain_second.reshape(1, 96), conv_second.reshape(9, 288, 192), shortcut,
    )
    return latents.reshape(2, 4, 32, 1, 768)


def solution(mesh):
    sizes = (mesh.shape["rows"], mesh.shape["tm"], mesh.shape["clip"], 8)
    return jax.shard_map(
        functools.partial(shards, sizes),
        mesh=mesh,
        in_specs=(P("clip", "tm", "rows", None, None), P(), P(), P(), P(), P(), P()),
        out_specs=P(None, "tm", None, ("rows", "clip"), None),
        check_vma=False,
    )
```

```python
import functools

import jax
import jax.numpy as jnp
from jax import lax
from jax.experimental import pallas as pl
from jax.experimental.pallas import tpu as pltpu
from jax.sharding import PartitionSpec as P

MESH = pl.DeviceIdType.MESH
F32 = jnp.float32
BF16 = jnp.bfloat16
VMEM_LIMIT = 56 * 1024 * 1024


def iota2(shape, dim):
    return lax.broadcasted_iota(jnp.int32, shape, dim)


def selector(rows, cols, offset):
    return jnp.where(iota2((rows, cols), 1) == iota2((rows, cols), 0) + offset, 1.0, 0.0).astype(BF16)


def dot(a, b):
    return jnp.dot(a, b, preferred_element_type=F32)


def place_exact(vector, chosen):
    wide = jnp.broadcast_to(vector, (8, vector.shape[1]))
    high = wide.astype(BF16)
    rest = wide - high.astype(F32)
    middle = rest.astype(BF16)
    low = (rest - middle.astype(F32)).astype(BF16)
    return (dot(high, chosen) + dot(middle, chosen) + dot(low, chosen))[0:1]


def squares_split(values):
    square = values * values
    high = square.astype(BF16)
    low = (square - high.astype(F32)).astype(BF16)
    return jnp.concatenate([high, low], 1)


def normsilu(values, meansq, half_gain):
    half = values * lax.rsqrt(meansq + 1e-6) * half_gain
    return half + half * jnp.tanh(half)


def shift_down(x):
    moved = pltpu.roll(x, 1, 0)
    return jnp.where(iota2(x.shape, 0) == 0, 0.0, moved)


def shift_up(x):
    rows = x.shape[0]
    moved = pltpu.roll(x, rows - 1, 0)
    return jnp.where(iota2(x.shape, 0) == rows - 1, 0.0, moved)


def packed(cells):
    c0, c1, c2, c3 = cells
    lane = iota2(c0.shape, 1)
    c1, c2, c3 = pltpu.roll(c1, 96, 1), pltpu.roll(c2, 64, 1), pltpu.roll(c3, 32, 1)
    return jnp.concatenate(
        [jnp.where(lane < 96, c0, c1), jnp.where(lane < 64, c1, c2), jnp.where(lane < 32, c2, c3)], 1)


def group_of(lane):
    left = jnp.where(lane < 416, 2, 4)
    right = jnp.where(lane < 608, 5, 1)
    return jnp.where(lane < 384, lane // 96, jnp.where(lane < 512, left, right))


def channel_of(lane):
    left = jnp.where(lane < 416, lane - 384 + 64, lane - 416)
    right = jnp.where(lane < 608, lane - 512, lane - 608)
    return jnp.where(lane < 384, lane % 96, jnp.where(lane < 512, left, right))


def encoder_kernel(
    sizes,
    video_hbm, gain1_hbm, w1_hbm, wd_hbm, gain2_hbm, w2_hbm, shortcut_hbm,
    out,
    video, gain1, w1, wd, gain2, w2, shortcut,
    ones1, ones2, gain_lanes2,
    past_video, cells1, cellsv, wdp, products, w5, part_out, part_in, own_sum,
    z_out, z_in, yc_wide, yc_out, yc_in,
    tiles, windows, raw, wa2, wb2, wsa, wsb,
    near_send, near_recv, z_send, z_recv, yc_send, yc_recv, load,
):
    row_total, tm_total, clip_total, z_total = sizes
    y_total = row_total // z_total
    square = y_total * clip_total
    tm = lax.axis_index("tm")
    row = lax.axis_index("rows")
    clip = lax.axis_index("clip")
    z, y = row // y_total, row % y_total
    spot = y * clip_total + clip
    has_up, has_down = row > 0, row < row_total - 1
    has_past, has_next = tm > 0, tm < tm_total - 1
    up, down = (tm, row - 1, clip), (tm, row + 1, clip)
    past, after = (tm - 1, row, clip), (tm + 1, row, clip)

    def z_partner(step):
        other = (z + step) % z_total
        return other, (tm, other * y_total + y, clip)

    def square_partner(step):
        other = (spot + step) % square
        return other, (tm, z * y_total + other // clip_total, other % clip_total)

    barrier = pltpu.get_barrier_semaphore()
    for exists, who in ((has_up, up), (has_down, down), (has_past, past), (has_next, after)):
        @pl.when(exists)
        def _():
            pl.semaphore_signal(barrier, inc=1, device_id=who, device_id_type=MESH)
    for step in range(1, z_total):
        pl.semaphore_signal(barrier, inc=1, device_id=z_partner(step)[1], device_id_type=MESH)
    for step in range(1, square):
        pl.semaphore_signal(barrier, inc=1, device_id=square_partner(step)[1], device_id_type=MESH)

    loads = [
        pltpu.make_async_copy(src, dst, load.at[n])
        for n, (src, dst) in enumerate((
            (video_hbm, video), (gain1_hbm, gain1), (w1_hbm, w1), (wd_hbm, wd),
            (gain2_hbm, gain2), (w2_hbm, w2), (shortcut_hbm, shortcut)))]
    for one in loads:
        one.start()

    def remote(src, dst, index, who):
        return pltpu.make_async_remote_copy(
            src_ref=src, dst_ref=dst, send_sem=near_send.at[index], recv_sem=near_recv.at[index],
            device_id=who, device_id_type=MESH)

    frames = remote(video_hbm.at[2:4], past_video, 0, after)
    ups = [remote(part_out.at[0, n], part_in.at[0, n], 1 + n, up) for n in range(2)]
    downs = [remote(part_out.at[1, n], part_in.at[1, n], 3 + n, down) for n in range(2)]
    later = remote(windows.at[1, 4:6], windows.at[1, 0:2], 5, after)

    def when(condition, *steps):
        @pl.when(condition)
        def _():
            for step in steps:
                step()

    ones1[...] = jnp.where(
        iota2((768, 384), 0) % 384 // 96 == iota2((768, 384), 1) // 96, 1.0, 0.0).astype(BF16)
    line = iota2((128, 128), 0)
    order = jnp.where(
        iota2((128, 128), 1) == jnp.where(line < 64, 2 * line, 2 * line - 127), 1.0, 0.0).astype(BF16)
    loads[1].wait()
    gain_lanes1 = 0.5 * place_exact(
        gain1[...], jnp.where(iota2((96, 384), 1) % 96 == iota2((96, 384), 0), 1.0, 0.0).astype(BF16))
    loads[0].wait()

    lane64 = iota2((64, 128), 1)
    line64 = iota2((64, 128), 0)

    def windows_of(even, odd):
        return shift_up(even[:, 0:128]), shift_up(even[:, 128:256]), shift_down(odd[:, 256:384])

    def spread_first(t, r, even, odd):
        after0, after1, before2 = windows_of(even, odd)
        last = jnp.where(line64 == 63, pltpu.roll(odd[:, 256:384], 32, 1), 0.0)
        cells1[t, r, 0] = jnp.concatenate([
            even, odd[:, 0:128], jnp.where(lane64 < 64, odd[:, 128:256], 0.0),
            jnp.where(lane64 < 32, 0.0, before2)], 1).astype(BF16)
        cells1[t, r, 1] = jnp.concatenate([
            odd, after0, jnp.where(lane64 < 64, after1, last),
            jnp.where(lane64 < 32, last, even[:, 256:384])], 1).astype(BF16)

    def norm_first(t, source, f):
        values = jnp.concatenate([dot(order, source[f, 0]), dot(order, source[f, 1])], 0)
        meansq = dot(squares_split(values), ones1[...]) * (1.0 / 96.0)
        result = normsilu(values, meansq, gain_lanes1)
        for r in range(2):
            even, odd = result[128 * r:128 * r + 64], result[128 * r + 64:128 * r + 128]
            spread_first(t, r, even, odd)
        return values

    def norm_own(t):
        values = norm_first(t + 2, video, t)
        for r in range(2):
            even, odd = values[128 * r:128 * r + 64], values[128 * r + 64:128 * r + 128]
            cellsv[t, r, 0] = jnp.concatenate([even, odd[:, 0:128]], 1).astype(BF16)
            cellsv[t, r, 1] = jnp.concatenate([odd, shift_up(even[:, 0:128])], 1).astype(BF16)

    for t in range(4):
        norm_own(t)

    count = has_up.astype(jnp.int32) + has_down.astype(jnp.int32) + has_past.astype(jnp.int32) + has_next.astype(jnp.int32)
    pl.semaphore_wait(barrier, count + (z_total - 1) + (square - 1))
    when(has_next, frames.start)

    @pl.when(jnp.logical_not(has_up))
    def _():
        part_in[1] = jnp.zeros((2, 128, 384), BF16)

    @pl.when(jnp.logical_not(has_down))
    def _():
        part_in[0] = jnp.zeros((2, 128, 384), BF16)

    @pl.when(jnp.logical_not(has_past))
    def _():
        past_video[...] = jnp.zeros((2, 2, 128, 384), BF16)
        windows[1, 0:2] = jnp.zeros((2, 64, 640), BF16)

    loads[3].wait()
    wdp[...] = jnp.zeros((96, 1152), BF16)
    for i in range(3):
        for j in range(3):
            wdp[:, 128 * (3 * i + j):128 * (3 * i + j) + 96] = wd[i, 96 * j:96 * j + 96]
    blank = jnp.zeros((96, 128), F32)

    def down_tap(i, j):
        return wdp[:, 128 * (3 * i + j):128 * (3 * i + j) + 128]

    for r, i in ((1, 0), (2, 1), (3, 2)):
        none = blank.astype(BF16)
        for n, (q0, q1) in enumerate((
                (down_tap(i, 0), none), (down_tap(i, 1), none), (down_tap(i, 2), down_tap(i, 0)),
                (none, down_tap(i, 1)), (none, down_tap(i, 2)))):
            w5[r, 2304 + 96 * n:2400 + 96 * n] = jnp.concatenate([q0, q1], 1)
        w5[r, 2784:2816] = jnp.zeros((32, 256), BF16)
    below = has_down.astype(F32)
    loads[2].wait()

    def compose_step(a, carry):
        for i in range(3):
            products[i] = dot(w1[3 * a + i], wdp[...])

        def total(r, pairs):
            result = None
            for i in range(3):
                lower = r - i
                if 0 <= lower <= 2:
                    for j, across in pairs:
                        lane = 128 * (3 * lower + across)
                        term = products[i, 96 * j:96 * j + 96, lane:lane + 128]
                        if r == 2 and lower == 2:
                            term = term * below
                        result = term if result is None else result + term
            return result

        start = pl.multiple_of(a * 768, 128)
        for r in range(5):
            at = [total(r, [(j, c - j) for j in range(3) if 0 <= c - j <= 2]) for c in range(5)]
            beyond = -total(r, [(0, 2)])
            for n, (q0, q1) in enumerate((
                    (at[1], blank), (at[2], at[0]), (at[3], at[1]), (at[4], at[2]),
                    (blank, at[3]), (blank, at[4]), (blank, beyond), (at[0], blank))):
                w5[r, pl.ds(start + 96 * n, 96)] = jnp.concatenate([q0, q1], 1).astype(BF16)
        return carry

    lax.fori_loop(0, 3, compose_step, 0)

    def row_cells(t, r, with_video):
        pieces = [cells1[t + a:t + a + 2, r].reshape(256, 768) for a in range(3)]
        if with_video:
            pieces.append(cellsv[t:t + 2, r].reshape(256, 512))
        return jnp.concatenate(pieces, 1)

    def compact(total):
        frames_here = []
        for f in range(2):
            base = 128 * f
            frames_here.append(packed([
                total[base + 64 * p:base + 64 * p + 64, 128 * q:128 * q + 128]
                for p in range(2) for q in range(2)]))
        return jnp.concatenate(frames_here, 0)

    def send_partials(half, t):
        total = dot(row_cells(t, 0, True), w5[3]) + dot(row_cells(t, 1, False), w5[4, 0:2304])
        part_out[0, half] = compact(total).astype(BF16)
        when(has_up, ups[half].start)
        part_out[1, half] = compact(dot(row_cells(t, 1, False), w5[0, 0:2304])).astype(BF16)
        when(has_down, downs[half].start)

    def sum_own(half, t):
        total = dot(row_cells(t, 0, True), w5[1]) + dot(row_cells(t, 1, True), w5[2])
        own_sum[half] = compact(total)

    def reduce_half(half):
        when(has_down, ups[half].wait_recv)
        when(has_up, downs[half].wait_recv)
        total = own_sum[half] + part_in[0, half].astype(F32) + part_in[1, half].astype(F32)
        total = total.astype(BF16).astype(F32)
        spot_in_block = iota2((64, 128), 0) % 8
        wide = []
        for f in range(2):
            cell = total[64 * f:64 * f + 64]
            edge = jnp.where(spot_in_block < 4, shift_down(cell[:, 256:384]), shift_up(cell[:, 0:128]))
            wide.append(jnp.concatenate([cell, edge], 1).reshape(z_total, 8, 512))
        z_out[half] = jnp.concatenate(wide, 1).astype(BF16)

    def z_copy(half, step, arriving):
        other, who = z_partner(step)
        here = (z - step + z_total) % z_total
        slot = half * z_total + step
        return pltpu.make_async_remote_copy(
            src_ref=z_out.at[half, other], dst_ref=z_in.at[half, here if arriving else z],
            send_sem=z_send.at[slot], recv_sem=z_recv.at[slot], device_id=who, device_id_type=MESH)

    def send_z(half):
        for step in range(1, z_total):
            z_copy(half, step, False).start()
        z_in[half, z] = z_out[half, z]

    send_partials(0, 2)
    sum_own(0, 2)

    def halo_frames():
        frames.wait_recv()

    when(has_past, halo_frames)
    for t in range(2):
        norm_first(t, past_video, t)
    send_partials(1, 0)
    reduce_half(0)
    send_z(0)
    sum_own(1, 0)

    lane2 = iota2((192, 768), 1)
    source2 = iota2((192, 768), 0)
    places2 = jnp.where(lane2 == jnp.where(lane2 < 384, source2, source2 + 576), 1.0, 0.0).astype(BF16)
    loads[5].wait()

    def weight2_step(tap, carry):
        placed = dot(w2[tap], places2)
        p0, p1 = placed[:, 0:384], placed[:, 384:768]
        wa2[tap, 0:96] = (p0[96:192] + p1[0:96]).astype(BF16)
        wa2[tap, 96:192] = (p0[192:288] + p1[96:192]).astype(BF16)
        wa2[tap, 192:288] = p1[192:288].astype(BF16)
        wa2[tap, 288:384] = p0[0:96].astype(BF16)
        wb2[tap, 0:96] = p1[192:288].astype(BF16)
        wb2[tap, 96:192] = p0[0:96].astype(BF16)
        wb2[tap, 192:288] = (p0[96:192] + p1[0:96]).astype(BF16)
        wb2[tap, 288:384] = (p0[192:288] + p1[96:192]).astype(BF16)
        return carry

    lax.fori_loop(0, 9, weight2_step, 0)

    loads[6].wait()
    placed2 = dot(shortcut[...], places2).astype(BF16)
    wsa[0:96] = placed2[:, 0:384]
    wsa[96:192] = placed2[:, 384:768]
    wsa[192:384] = jnp.zeros((192, 384), BF16)
    wsb[0:192] = jnp.zeros((192, 384), BF16)
    wsb[192:288] = placed2[:, 0:384]
    wsb[288:384] = placed2[:, 384:768]
    rows640 = iota2((640, 640), 0)
    twice = jnp.logical_or(jnp.logical_and(rows640 >= 384, rows640 < 416), rows640 >= 608)
    from_group = jnp.where(twice, -1, group_of(rows640))
    same = jnp.where(from_group == group_of(iota2((640, 640), 1)), 1.0, 0.0).astype(BF16)
    ones2[0:640] = same
    ones2[640:1280] = same
    loads[4].wait()
    gain_lanes2[...] = jnp.broadcast_to(0.5 * place_exact(gain2[...], jnp.where(
        channel_of(iota2((96, 640), 1)) == iota2((96, 640), 0), 1.0, 0.0).astype(BF16)), (8, 640))

    reduce_half(1)
    send_z(1)

    def yc_copy(half, step, arriving):
        other, who = square_partner(step)
        here = (spot - step + square) % square
        slot = half * square + step
        return pltpu.make_async_remote_copy(
            src_ref=yc_out.at[half, other], dst_ref=yc_in.at[half, here if arriving else spot],
            send_sem=yc_send.at[slot], recv_sem=yc_recv.at[slot], device_id=who, device_id_type=MESH)

    lane8 = iota2((8, 128), 1)
    line8 = iota2((8, 128), 0)

    def relay(half):
        for step in range(1, z_total):
            z_copy(half, step, True).wait_recv()
        for source in range(z_total):
            cells = z_in[half, source].astype(F32)
            for f in range(2):
                cell = cells[8 * f:8 * f + 8]
                t0, t1, t2, edge = (cell[:, 128 * n:128 * n + 128] for n in range(4))
                before = jnp.where(line8 == 0, edge, pltpu.roll(t2, 1, 0))
                following = jnp.where(line8 == 7, edge, pltpu.roll(t0, 7, 0))
                parts = (t0, t1, t2, jnp.where(lane8 < 32, t2, before), jnp.where(lane8 < 96, following, t0))
                for n, part in enumerate(parts):
                    yc_wide[n, pl.ds(f * 8 + source, 8, stride=16), :] = part
        for n in range(5):
            yc_out[half, :, :, 128 * n:128 * n + 128] = yc_wide[n].astype(BF16).reshape(8, 16, 128)
        for step in range(1, square):
            yc_copy(half, step, False).start()
        yc_in[half, spot] = yc_out[half, spot]

    relay(0)
    relay(1)

    def norm_second(half, t):
        for step in range(1, square):
            yc_copy(half, step, True).wait_recv()
        for source in range(square):
            cells = yc_in[half, source].astype(F32)
            start = (source % clip_total) * row_total + source // clip_total
            for f in range(2):
                for n in range(5):
                    tiles[n, pl.ds(64 * f + start, 8, stride=y_total), :] = cells[8 * f:8 * f + 8, 128 * n:128 * n + 128]
        values = jnp.concatenate([tiles[n] for n in range(5)], 1)
        raw[t:t + 2] = values[:, 0:384].astype(BF16).reshape(2, 64, 384)
        meansq = dot(squares_split(values), ones2[...]) * (1.0 / 96.0)
        second = normsilu(values, meansq, gain_lanes2[0:1])
        windows[1, t + 2:t + 4] = second.astype(BF16).reshape(2, 64, 640)
        return second

    def shifted(second, t):
        line = iota2((128, 640), 0) % 32
        windows[0, t:t + 2] = jnp.where(line == 0, 0.0, pltpu.roll(second, 1, 0)).astype(BF16).reshape(2, 64, 640)
        windows[2, t:t + 2] = jnp.where(line == 31, 0.0, pltpu.roll(second, 127, 0)).astype(BF16).reshape(2, 64, 640)

    second = norm_second(0, 2)
    when(has_next, later.start)
    shifted(second, 4)
    second = norm_second(1, 0)
    shifted(second, 2)
    when(has_past, later.wait_recv)
    shifted(windows[1, 0:2].reshape(128, 640).astype(F32), 0)

    def conv(weights, direct, lane_sets):
        acc = dot(raw[...].reshape(256, 384), direct[...])
        for a in range(3):
            pieces = []
            for i in range(3):
                pieces += [windows[i, a:a + 4, :, lo:hi].reshape(256, hi - lo) for lo, hi in lane_sets]
            acc += dot(jnp.concatenate(pieces, 1), weights[3 * a:3 * a + 3].reshape(1152, 384))
        return acc.astype(BF16).reshape(4, 2, 32, 384)

    left = conv(wa2, wsa, ((0, 256), (384, 512)))
    for c in range(2):
        out[c, :, :, 0:384] = left[:, c]
    right = conv(wb2, wsb, ((512, 640), (128, 384)))
    for c in range(2):
        out[c, :, :, 384:768] = right[:, c]

    when(has_up, ups[0].wait_send, ups[1].wait_send)
    when(has_down, downs[0].wait_send, downs[1].wait_send)
    when(has_next, frames.wait_send, later.wait_send)
    for half in range(2):
        for step in range(1, z_total):
            z_copy(half, step, False).wait_send()
        for step in range(1, square):
            yc_copy(half, step, False).wait_send()


def vmem(shape, dtype=BF16):
    return pltpu.VMEM(shape, dtype)


def shards(sizes, video, gain_first, conv_first, down, gain_second, conv_second, shortcut):
    dma = pltpu.SemaphoreType.DMA
    latents = pl.pallas_call(
        functools.partial(encoder_kernel, sizes),
        out_shape=jax.ShapeDtypeStruct((2, 4, 32, 768), BF16),
        in_specs=[pl.BlockSpec(memory_space=pl.ANY)] * 7,
        out_specs=pl.BlockSpec(memory_space=pltpu.VMEM),
        scratch_shapes=[
            vmem((4, 2, 128, 384)), vmem((1, 96), F32), vmem((9, 288, 96)), vmem((3, 288, 96)),
            vmem((1, 96), F32), vmem((9, 288, 192)), vmem((96, 192)),
            vmem((768, 384)), vmem((1280, 640)), vmem((8, 640), F32),
            vmem((2, 2, 128, 384)), vmem((6, 2, 2, 64, 768)), vmem((4, 2, 2, 64, 512)),
            vmem((96, 1152)), vmem((3, 288, 1152), F32), vmem((5, 2816, 256)),
            vmem((2, 2, 128, 384)), vmem((2, 2, 128, 384)), vmem((2, 128, 384), F32),
            vmem((2, 8, 16, 512)), vmem((2, 8, 16, 512)),
            vmem((5, 128, 128), F32), vmem((2, 8, 16, 640)), vmem((2, 8, 16, 640)),
            vmem((5, 128, 128), F32), vmem((3, 6, 64, 640)), vmem((4, 64, 384)),
            vmem((9, 384, 384)), vmem((9, 384, 384)), vmem((384, 384)), vmem((384, 384)),
            dma((6,)), dma((6,)), dma((16,)), dma((16,)), dma((16,)), dma((16,)), dma((7,)),
        ],
        compiler_params=pltpu.CompilerParams(
            collective_id=0, has_side_effects=True, vmem_limit_bytes=VMEM_LIMIT),
        name="encoder",
    )(
        video.reshape(4, 2, 128, 384), gain_first.reshape(1, 96),
        conv_first.reshape(9, 288, 96), down.reshape(3, 288, 96),
        gain_second.reshape(1, 96), conv_second.reshape(9, 288, 192), shortcut,
    )
    return latents.reshape(2, 4, 32, 1, 768)


def solution(mesh):
    sizes = (mesh.shape["rows"], mesh.shape["tm"], mesh.shape["clip"], 8)
    return jax.shard_map(
        functools.partial(shards, sizes),
        mesh=mesh,
        in_specs=(P("clip", "tm", "rows", None, None), P(), P(), P(), P(), P(), P()),
        out_specs=P(None, "tm", None, ("rows", "clip"), None),
        check_vma=False,
    )
```

```python
import functools

import jax
import jax.numpy as jnp
from jax import lax
from jax.experimental import pallas as pl
from jax.experimental.pallas import tpu as pltpu
from jax.sharding import PartitionSpec as P

MESH = pl.DeviceIdType.MESH
F32 = jnp.float32
BF16 = jnp.bfloat16
VMEM_LIMIT = 56 * 1024 * 1024


def iota2(shape, dim):
    return lax.broadcasted_iota(jnp.int32, shape, dim)


def selector(rows, cols, offset):
    return jnp.where(iota2((rows, cols), 1) == iota2((rows, cols), 0) + offset, 1.0, 0.0).astype(BF16)


def dot(a, b):
    return jnp.dot(a, b, preferred_element_type=F32)


def place_exact(vector, chosen):
    wide = jnp.broadcast_to(vector, (8, vector.shape[1]))
    high = wide.astype(BF16)
    rest = wide - high.astype(F32)
    middle = rest.astype(BF16)
    low = (rest - middle.astype(F32)).astype(BF16)
    return (dot(high, chosen) + dot(middle, chosen) + dot(low, chosen))[0:1]


def squares_split(values):
    square = values * values
    high = square.astype(BF16)
    low = (square - high.astype(F32)).astype(BF16)
    return jnp.concatenate([high, low], 1)


def normsilu(values, meansq, half_gain):
    half = values * lax.rsqrt(meansq + 1e-6) * half_gain
    return half + half * jnp.tanh(half)


def shift_down(x):
    moved = pltpu.roll(x, 1, 0)
    return jnp.where(iota2(x.shape, 0) == 0, 0.0, moved)


def shift_up(x):
    rows = x.shape[0]
    moved = pltpu.roll(x, rows - 1, 0)
    return jnp.where(iota2(x.shape, 0) == rows - 1, 0.0, moved)


def packed(cells):
    c0, c1, c2, c3 = cells
    lane = iota2(c0.shape, 1)
    c1, c2, c3 = pltpu.roll(c1, 96, 1), pltpu.roll(c2, 64, 1), pltpu.roll(c3, 32, 1)
    return jnp.concatenate(
        [jnp.where(lane < 96, c0, c1), jnp.where(lane < 64, c1, c2), jnp.where(lane < 32, c2, c3)], 1)


def group_of(lane):
    left = jnp.where(lane < 416, 2, 4)
    right = jnp.where(lane < 608, 5, 1)
    return jnp.where(lane < 384, lane // 96, jnp.where(lane < 512, left, right))


def channel_of(lane):
    left = jnp.where(lane < 416, lane - 384 + 64, lane - 416)
    right = jnp.where(lane < 608, lane - 512, lane - 608)
    return jnp.where(lane < 384, lane % 96, jnp.where(lane < 512, left, right))


def encoder_kernel(
    sizes,
    video_hbm, gain1_hbm, w1_hbm, wd_hbm, gain2_hbm, w2_hbm, shortcut_hbm,
    out,
    video, gain1, w1, wd, gain2, w2, shortcut,
    ones1, ones2, gain_lanes2,
    past_video, cells1, cellsv, wdp, products, w5, part_out, part_in, own_sum,
    z_out, z_in, yc_wide, yc_out, yc_in,
    tiles, windows, raw, wa2, wb2, wsa, wsb,
    near_send, near_recv, z_send, z_recv, yc_send, yc_recv, load,
):
    row_total, tm_total, clip_total, z_total = sizes
    y_total = row_total // z_total
    square = y_total * clip_total
    tm = lax.axis_index("tm")
    row = lax.axis_index("rows")
    clip = lax.axis_index("clip")
    z, y = row // y_total, row % y_total
    spot = y * clip_total + clip
    has_up, has_down = row > 0, row < row_total - 1
    has_past, has_next = tm > 0, tm < tm_total - 1
    up, down = (tm, row - 1, clip), (tm, row + 1, clip)
    past, after = (tm - 1, row, clip), (tm + 1, row, clip)

    def z_partner(step):
        other = (z + step) % z_total
        return other, (tm, other * y_total + y, clip)

    def square_partner(step):
        other = (spot + step) % square
        return other, (tm, z * y_total + other // clip_total, other % clip_total)

    barrier = pltpu.get_barrier_semaphore()
    for exists, who in ((has_up, up), (has_down, down), (has_past, past), (has_next, after)):
        @pl.when(exists)
        def _():
            pl.semaphore_signal(barrier, inc=1, device_id=who, device_id_type=MESH)
    for step in range(1, z_total):
        pl.semaphore_signal(barrier, inc=1, device_id=z_partner(step)[1], device_id_type=MESH)
    for step in range(1, square):
        pl.semaphore_signal(barrier, inc=1, device_id=square_partner(step)[1], device_id_type=MESH)

    loads = [
        pltpu.make_async_copy(src, dst, load.at[n])
        for n, (src, dst) in enumerate((
            (video_hbm, video), (gain1_hbm, gain1), (w1_hbm, w1), (wd_hbm, wd),
            (gain2_hbm, gain2), (w2_hbm, w2), (shortcut_hbm, shortcut)))]
    for one in loads:
        one.start()

    def remote(src, dst, index, who):
        return pltpu.make_async_remote_copy(
            src_ref=src, dst_ref=dst, send_sem=near_send.at[index], recv_sem=near_recv.at[index],
            device_id=who, device_id_type=MESH)

    frames = remote(video_hbm.at[2:4], past_video, 0, after)
    ups = [remote(part_out.at[0, n], part_in.at[0, n], 1 + n, up) for n in range(2)]
    downs = [remote(part_out.at[1, n], part_in.at[1, n], 3 + n, down) for n in range(2)]
    later = remote(windows.at[1, 4:6], windows.at[1, 0:2], 5, after)

    def when(condition, *steps):
        @pl.when(condition)
        def _():
            for step in steps:
                step()

    ones1[...] = jnp.where(
        iota2((768, 384), 0) % 384 // 96 == iota2((768, 384), 1) // 96, 1.0, 0.0).astype(BF16)
    line = iota2((128, 128), 0)
    order = jnp.where(
        iota2((128, 128), 1) == jnp.where(line < 64, 2 * line, 2 * line - 127), 1.0, 0.0).astype(BF16)
    loads[1].wait()
    gain_lanes1 = 0.5 * place_exact(
        gain1[...], jnp.where(iota2((96, 384), 1) % 96 == iota2((96, 384), 0), 1.0, 0.0).astype(BF16))
    loads[0].wait()

    lane64 = iota2((64, 128), 1)
    line64 = iota2((64, 128), 0)

    def windows_of(even, odd):
        return shift_up(even[:, 0:128]), shift_up(even[:, 128:256]), shift_down(odd[:, 256:384])

    def spread_first(t, r, even, odd):
        after0, after1, before2 = windows_of(even, odd)
        last = jnp.where(line64 == 63, pltpu.roll(odd[:, 256:384], 32, 1), 0.0)
        cells1[t, r, 0] = jnp.concatenate([
            even, odd[:, 0:128], jnp.where(lane64 < 64, odd[:, 128:256], 0.0),
            jnp.where(lane64 < 32, 0.0, before2)], 1).astype(BF16)
        cells1[t, r, 1] = jnp.concatenate([
            odd, after0, jnp.where(lane64 < 64, after1, last),
            jnp.where(lane64 < 32, last, even[:, 256:384])], 1).astype(BF16)

    def norm_first(t, source, f):
        values = jnp.concatenate([dot(order, source[f, 0]), dot(order, source[f, 1])], 0)
        meansq = dot(squares_split(values), ones1[...]) * (1.0 / 96.0)
        result = normsilu(values, meansq, gain_lanes1)
        for r in range(2):
            even, odd = result[128 * r:128 * r + 64], result[128 * r + 64:128 * r + 128]
            spread_first(t, r, even, odd)
        return values

    def norm_own(t):
        values = norm_first(t + 2, video, t)
        for r in range(2):
            even, odd = values[128 * r:128 * r + 64], values[128 * r + 64:128 * r + 128]
            cellsv[t, r, 0] = jnp.concatenate([even, odd[:, 0:128]], 1).astype(BF16)
            cellsv[t, r, 1] = jnp.concatenate([odd, shift_up(even[:, 0:128])], 1).astype(BF16)

    for t in range(4):
        norm_own(t)

    count = has_up.astype(jnp.int32) + has_down.astype(jnp.int32) + has_past.astype(jnp.int32) + has_next.astype(jnp.int32)
    pl.semaphore_wait(barrier, count + (z_total - 1) + (square - 1))
    when(has_next, frames.start)

    @pl.when(jnp.logical_not(has_up))
    def _():
        part_in[1] = jnp.zeros((2, 128, 384), BF16)

    @pl.when(jnp.logical_not(has_down))
    def _():
        part_in[0] = jnp.zeros((2, 128, 384), BF16)

    @pl.when(jnp.logical_not(has_past))
    def _():
        past_video[...] = jnp.zeros((2, 2, 128, 384), BF16)
        windows[1, 0:2] = jnp.zeros((2, 64, 640), BF16)

    loads[3].wait()
    wdp[...] = jnp.zeros((96, 1152), BF16)
    for i in range(3):
        for j in range(3):
            wdp[:, 128 * (3 * i + j):128 * (3 * i + j) + 96] = wd[i, 96 * j:96 * j + 96]
    blank = jnp.zeros((96, 128), F32)

    def down_tap(i, j):
        return wdp[:, 128 * (3 * i + j):128 * (3 * i + j) + 128]

    for r, i in ((1, 0), (2, 1), (3, 2)):
        none = blank.astype(BF16)
        for n, (q0, q1) in enumerate((
                (down_tap(i, 0), none), (down_tap(i, 1), none), (down_tap(i, 2), down_tap(i, 0)),
                (none, down_tap(i, 1)), (none, down_tap(i, 2)))):
            w5[r, 2304 + 96 * n:2400 + 96 * n] = jnp.concatenate([q0, q1], 1)
        w5[r, 2784:2816] = jnp.zeros((32, 256), BF16)
    below = has_down.astype(F32)
    loads[2].wait()

    def compose_step(a, carry):
        for i in range(3):
            products[i] = dot(w1[3 * a + i], wdp[...])

        def total(r, pairs):
            result = None
            for i in range(3):
                lower = r - i
                if 0 <= lower <= 2:
                    for j, across in pairs:
                        lane = 128 * (3 * lower + across)
                        term = products[i, 96 * j:96 * j + 96, lane:lane + 128]
                        if r == 2 and lower == 2:
                            term = term * below
                        result = term if result is None else result + term
            return result

        start = a * 768
        for r in range(5):
            at = [total(r, [(j, c - j) for j in range(3) if 0 <= c - j <= 2]) for c in range(5)]
            beyond = -total(r, [(0, 2)])
            for n, (q0, q1) in enumerate((
                    (at[1], blank), (at[2], at[0]), (at[3], at[1]), (at[4], at[2]),
                    (blank, at[3]), (blank, at[4]), (blank, beyond), (at[0], blank))):
                w5[r, pl.ds(start + 96 * n, 96)] = jnp.concatenate([q0, q1], 1).astype(BF16)
        return carry

    for a in range(3):
        compose_step(a, 0)

    def row_cells(t, r, with_video):
        pieces = [cells1[t + a:t + a + 2, r].reshape(256, 768) for a in range(3)]
        if with_video:
            pieces.append(cellsv[t:t + 2, r].reshape(256, 512))
        return jnp.concatenate(pieces, 1)

    def compact(total):
        frames_here = []
        for f in range(2):
            base = 128 * f
            frames_here.append(packed([
                total[base + 64 * p:base + 64 * p + 64, 128 * q:128 * q + 128]
                for p in range(2) for q in range(2)]))
        return jnp.concatenate(frames_here, 0)

    def send_partials(half, t):
        total = dot(row_cells(t, 0, True), w5[3]) + dot(row_cells(t, 1, False), w5[4, 0:2304])
        part_out[0, half] = compact(total).astype(BF16)
        when(has_up, ups[half].start)
        part_out[1, half] = compact(dot(row_cells(t, 1, False), w5[0, 0:2304])).astype(BF16)
        when(has_down, downs[half].start)

    def sum_own(half, t):
        total = dot(row_cells(t, 0, True), w5[1]) + dot(row_cells(t, 1, True), w5[2])
        own_sum[half] = compact(total)

    def reduce_half(half):
        when(has_down, ups[half].wait_recv)
        when(has_up, downs[half].wait_recv)
        total = own_sum[half] + part_in[0, half].astype(F32) + part_in[1, half].astype(F32)
        total = total.astype(BF16).astype(F32)
        spot_in_block = iota2((64, 128), 0) % 8
        wide = []
        for f in range(2):
            cell = total[64 * f:64 * f + 64]
            edge = jnp.where(spot_in_block < 4, shift_down(cell[:, 256:384]), shift_up(cell[:, 0:128]))
            wide.append(jnp.concatenate([cell, edge], 1).reshape(z_total, 8, 512))
        z_out[half] = jnp.concatenate(wide, 1).astype(BF16)

    def z_copy(half, step, arriving):
        other, who = z_partner(step)
        here = (z - step + z_total) % z_total
        slot = half * z_total + step
        return pltpu.make_async_remote_copy(
            src_ref=z_out.at[half, other], dst_ref=z_in.at[half, here if arriving else z],
            send_sem=z_send.at[slot], recv_sem=z_recv.at[slot], device_id=who, device_id_type=MESH)

    def send_z(half):
        for step in sorted(range(1, z_total), key=lambda step: -min(step, z_total - step)):
            z_copy(half, step, False).start()
        z_in[half, z] = z_out[half, z]

    send_partials(0, 2)
    sum_own(0, 2)

    def halo_frames():
        frames.wait_recv()

    when(has_past, halo_frames)
    for t in range(2):
        norm_first(t, past_video, t)
    send_partials(1, 0)
    reduce_half(0)
    send_z(0)
    sum_own(1, 0)

    lane2 = iota2((192, 768), 1)
    source2 = iota2((192, 768), 0)
    places2 = jnp.where(lane2 == jnp.where(lane2 < 384, source2, source2 + 576), 1.0, 0.0).astype(BF16)
    loads[5].wait()

    def weight2_step(tap, carry):
        placed = dot(w2[tap], places2)
        p0, p1 = placed[:, 0:384], placed[:, 384:768]
        wa2[tap, 0:96] = (p0[96:192] + p1[0:96]).astype(BF16)
        wa2[tap, 96:192] = (p0[192:288] + p1[96:192]).astype(BF16)
        wa2[tap, 192:288] = p1[192:288].astype(BF16)
        wa2[tap, 288:384] = p0[0:96].astype(BF16)
        wb2[tap, 0:96] = p1[192:288].astype(BF16)
        wb2[tap, 96:192] = p0[0:96].astype(BF16)
        wb2[tap, 192:288] = (p0[96:192] + p1[0:96]).astype(BF16)
        wb2[tap, 288:384] = (p0[192:288] + p1[96:192]).astype(BF16)
        return carry

    lax.fori_loop(0, 9, weight2_step, 0)

    loads[6].wait()
    placed2 = dot(shortcut[...], places2).astype(BF16)
    wsa[0:96] = placed2[:, 0:384]
    wsa[96:192] = placed2[:, 384:768]
    wsa[192:384] = jnp.zeros((192, 384), BF16)
    wsb[0:192] = jnp.zeros((192, 384), BF16)
    wsb[192:288] = placed2[:, 0:384]
    wsb[288:384] = placed2[:, 384:768]
    rows640 = iota2((640, 640), 0)
    twice = jnp.logical_or(jnp.logical_and(rows640 >= 384, rows640 < 416), rows640 >= 608)
    from_group = jnp.where(twice, -1, group_of(rows640))
    same = jnp.where(from_group == group_of(iota2((640, 640), 1)), 1.0, 0.0).astype(BF16)
    ones2[0:640] = same
    ones2[640:1280] = same
    loads[4].wait()
    gain_lanes2[...] = jnp.broadcast_to(0.5 * place_exact(gain2[...], jnp.where(
        channel_of(iota2((96, 640), 1)) == iota2((96, 640), 0), 1.0, 0.0).astype(BF16)), (8, 640))

    reduce_half(1)
    send_z(1)

    def yc_copy(half, step, arriving):
        other, who = square_partner(step)
        here = (spot - step + square) % square
        slot = half * square + step
        return pltpu.make_async_remote_copy(
            src_ref=yc_out.at[half, other], dst_ref=yc_in.at[half, here if arriving else spot],
            send_sem=yc_send.at[slot], recv_sem=yc_recv.at[slot], device_id=who, device_id_type=MESH)

    lane8 = iota2((8, 128), 1)
    line8 = iota2((8, 128), 0)

    def relay(half):
        for step in range(1, z_total):
            z_copy(half, step, True).wait_recv()
        for source in range(z_total):
            cells = z_in[half, source].astype(F32)
            for f in range(2):
                cell = cells[8 * f:8 * f + 8]
                t0, t1, t2, edge = (cell[:, 128 * n:128 * n + 128] for n in range(4))
                before = jnp.where(line8 == 0, edge, pltpu.roll(t2, 1, 0))
                following = jnp.where(line8 == 7, edge, pltpu.roll(t0, 7, 0))
                parts = (t0, t1, t2, jnp.where(lane8 < 32, t2, before), jnp.where(lane8 < 96, following, t0))
                for n, part in enumerate(parts):
                    yc_wide[n, pl.ds(f * 8 + source, 8, stride=16), :] = part
        for n in range(5):
            yc_out[half, :, :, 128 * n:128 * n + 128] = yc_wide[n].astype(BF16).reshape(8, 16, 128)
        for step in sorted(range(1, square), key=lambda step: -min(step, square - step)):
            yc_copy(half, step, False).start()
        yc_in[half, spot] = yc_out[half, spot]

    relay(0)
    relay(1)

    def norm_second(half, t):
        for step in range(1, square):
            yc_copy(half, step, True).wait_recv()
        for source in range(square):
            cells = yc_in[half, source].astype(F32)
            start = (source % clip_total) * row_total + source // clip_total
            for f in range(2):
                for n in range(5):
                    tiles[n, pl.ds(64 * f + start, 8, stride=y_total), :] = cells[8 * f:8 * f + 8, 128 * n:128 * n + 128]
        values = jnp.concatenate([tiles[n] for n in range(5)], 1)
        raw[t:t + 2] = values[:, 0:384].astype(BF16).reshape(2, 64, 384)
        meansq = dot(squares_split(values), ones2[...]) * (1.0 / 96.0)
        second = normsilu(values, meansq, gain_lanes2[0:1])
        windows[1, t + 2:t + 4] = second.astype(BF16).reshape(2, 64, 640)
        return second

    def shifted(second, t):
        line = iota2((128, 640), 0) % 32
        windows[0, t:t + 2] = jnp.where(line == 0, 0.0, pltpu.roll(second, 1, 0)).astype(BF16).reshape(2, 64, 640)
        windows[2, t:t + 2] = jnp.where(line == 31, 0.0, pltpu.roll(second, 127, 0)).astype(BF16).reshape(2, 64, 640)

    second = norm_second(0, 2)
    when(has_next, later.start)
    shifted(second, 4)
    second = norm_second(1, 0)
    shifted(second, 2)
    when(has_past, later.wait_recv)
    shifted(windows[1, 0:2].reshape(128, 640).astype(F32), 0)

    def conv(weights, direct, lane_sets):
        acc = dot(raw[...].reshape(256, 384), direct[...])
        for a in range(3):
            pieces = []
            for i in range(3):
                pieces += [windows[i, a:a + 4, :, lo:hi].reshape(256, hi - lo) for lo, hi in lane_sets]
            acc += dot(jnp.concatenate(pieces, 1), weights[3 * a:3 * a + 3].reshape(1152, 384))
        return acc.astype(BF16).reshape(4, 2, 32, 384)

    left = conv(wa2, wsa, ((0, 256), (384, 512)))
    for c in range(2):
        out[c, :, :, 0:384] = left[:, c]
    right = conv(wb2, wsb, ((512, 640), (128, 384)))
    for c in range(2):
        out[c, :, :, 384:768] = right[:, c]

    when(has_up, ups[0].wait_send, ups[1].wait_send)
    when(has_down, downs[0].wait_send, downs[1].wait_send)
    when(has_next, frames.wait_send, later.wait_send)
    for half in range(2):
        for step in range(1, z_total):
            z_copy(half, step, False).wait_send()
        for step in range(1, square):
            yc_copy(half, step, False).wait_send()


def vmem(shape, dtype=BF16):
    return pltpu.VMEM(shape, dtype)


def shards(sizes, video, gain_first, conv_first, down, gain_second, conv_second, shortcut):
    dma = pltpu.SemaphoreType.DMA
    latents = pl.pallas_call(
        functools.partial(encoder_kernel, sizes),
        out_shape=jax.ShapeDtypeStruct((2, 4, 32, 768), BF16),
        in_specs=[pl.BlockSpec(memory_space=pl.ANY)] * 7,
        out_specs=pl.BlockSpec(memory_space=pltpu.VMEM),
        scratch_shapes=[
            vmem((4, 2, 128, 384)), vmem((1, 96), F32), vmem((9, 288, 96)), vmem((3, 288, 96)),
            vmem((1, 96), F32), vmem((9, 288, 192)), vmem((96, 192)),
            vmem((768, 384)), vmem((1280, 640)), vmem((8, 640), F32),
            vmem((2, 2, 128, 384)), vmem((6, 2, 2, 64, 768)), vmem((4, 2, 2, 64, 512)),
            vmem((96, 1152)), vmem((3, 288, 1152), F32), vmem((5, 2816, 256)),
            vmem((2, 2, 128, 384)), vmem((2, 2, 128, 384)), vmem((2, 128, 384), F32),
            vmem((2, 8, 16, 512)), vmem((2, 8, 16, 512)),
            vmem((5, 128, 128), F32), vmem((2, 8, 16, 640)), vmem((2, 8, 16, 640)),
            vmem((5, 128, 128), F32), vmem((3, 6, 64, 640)), vmem((4, 64, 384)),
            vmem((9, 384, 384)), vmem((9, 384, 384)), vmem((384, 384)), vmem((384, 384)),
            dma((6,)), dma((6,)), dma((16,)), dma((16,)), dma((16,)), dma((16,)), dma((7,)),
        ],
        compiler_params=pltpu.CompilerParams(
            collective_id=0, has_side_effects=True, vmem_limit_bytes=VMEM_LIMIT),
        name="encoder",
    )(
        video.reshape(4, 2, 128, 384), gain_first.reshape(1, 96),
        conv_first.reshape(9, 288, 96), down.reshape(3, 288, 96),
        gain_second.reshape(1, 96), conv_second.reshape(9, 288, 192), shortcut,
    )
    return latents.reshape(2, 4, 32, 1, 768)


def solution(mesh):
    sizes = (mesh.shape["rows"], mesh.shape["tm"], mesh.shape["clip"], 8)
    return jax.shard_map(
        functools.partial(shards, sizes),
        mesh=mesh,
        in_specs=(P("clip", "tm", "rows", None, None), P(), P(), P(), P(), P(), P()),
        out_specs=P(None, "tm", None, ("rows", "clip"), None),
        check_vma=False,
    )
```

```python
import functools

import jax
import jax.numpy as jnp
from jax import lax
from jax.experimental import pallas as pl
from jax.experimental.pallas import tpu as pltpu
from jax.sharding import PartitionSpec as P

MESH = pl.DeviceIdType.MESH
F32 = jnp.float32
BF16 = jnp.bfloat16
VMEM_LIMIT = 56 * 1024 * 1024


def iota2(shape, dim):
    return lax.broadcasted_iota(jnp.int32, shape, dim)


def selector(rows, cols, offset):
    return jnp.where(iota2((rows, cols), 1) == iota2((rows, cols), 0) + offset, 1.0, 0.0).astype(BF16)


def dot(a, b):
    return jnp.dot(a, b, preferred_element_type=F32)


def place_exact(vector, chosen):
    wide = jnp.broadcast_to(vector, (8, vector.shape[1]))
    high = wide.astype(BF16)
    rest = wide - high.astype(F32)
    middle = rest.astype(BF16)
    low = (rest - middle.astype(F32)).astype(BF16)
    return (dot(high, chosen) + dot(middle, chosen) + dot(low, chosen))[0:1]


def squares_split(values):
    square = values * values
    high = square.astype(BF16)
    low = (square - high.astype(F32)).astype(BF16)
    return jnp.concatenate([high, low], 1)


def normsilu(values, meansq, half_gain):
    half = values * lax.rsqrt(meansq + 1e-6) * half_gain
    return half + half * jnp.tanh(half)


def shift_down(x):
    moved = pltpu.roll(x, 1, 0)
    return jnp.where(iota2(x.shape, 0) == 0, 0.0, moved)


def shift_up(x):
    rows = x.shape[0]
    moved = pltpu.roll(x, rows - 1, 0)
    return jnp.where(iota2(x.shape, 0) == rows - 1, 0.0, moved)


def packed(cells):
    c0, c1, c2, c3 = cells
    lane = iota2(c0.shape, 1)
    c1, c2, c3 = pltpu.roll(c1, 96, 1), pltpu.roll(c2, 64, 1), pltpu.roll(c3, 32, 1)
    return jnp.concatenate(
        [jnp.where(lane < 96, c0, c1), jnp.where(lane < 64, c1, c2), jnp.where(lane < 32, c2, c3)], 1)


def group_of(lane):
    left = jnp.where(lane < 416, 2, 4)
    right = jnp.where(lane < 608, 5, 1)
    return jnp.where(lane < 384, lane // 96, jnp.where(lane < 512, left, right))


def channel_of(lane):
    left = jnp.where(lane < 416, lane - 384 + 64, lane - 416)
    right = jnp.where(lane < 608, lane - 512, lane - 608)
    return jnp.where(lane < 384, lane % 96, jnp.where(lane < 512, left, right))


def encoder_kernel(
    sizes,
    video_hbm, gain1_hbm, w1_hbm, wd_hbm, gain2_hbm, w2_hbm, shortcut_hbm,
    out,
    video, gain1, w1, wd, gain2, w2, shortcut,
    ones1, ones2, gain_lanes2,
    past_video, cells1, cellsv, wdp, products, w5, part_out, part_in, own_sum,
    z_out, z_in, yc_wide, yc_out, yc_in,
    tiles, windows, raw, wa2, wb2, wsa, wsb,
    near_send, near_recv, z_send, z_recv, yc_send, yc_recv, load,
):
    row_total, tm_total, clip_total, z_total = sizes
    y_total = row_total // z_total
    square = y_total * clip_total
    tm = lax.axis_index("tm")
    row = lax.axis_index("rows")
    clip = lax.axis_index("clip")
    z, y = row // y_total, row % y_total
    spot = y * clip_total + clip
    has_up, has_down = row > 0, row < row_total - 1
    has_past, has_next = tm > 0, tm < tm_total - 1
    up, down = (tm, row - 1, clip), (tm, row + 1, clip)
    past, after = (tm - 1, row, clip), (tm + 1, row, clip)

    def z_partner(step):
        other = (z + step) % z_total
        return other, (tm, other * y_total + y, clip)

    def square_partner(step):
        other = (spot + step) % square
        return other, (tm, z * y_total + other // clip_total, other % clip_total)

    barrier = pltpu.get_barrier_semaphore()
    for exists, who in ((has_up, up), (has_down, down), (has_past, past), (has_next, after)):
        @pl.when(exists)
        def _():
            pl.semaphore_signal(barrier, inc=1, device_id=who, device_id_type=MESH)
    for step in range(1, z_total):
        pl.semaphore_signal(barrier, inc=1, device_id=z_partner(step)[1], device_id_type=MESH)
    for step in range(1, square):
        pl.semaphore_signal(barrier, inc=1, device_id=square_partner(step)[1], device_id_type=MESH)

    loads = [
        pltpu.make_async_copy(src, dst, load.at[n])
        for n, (src, dst) in enumerate((
            (video_hbm, video), (gain1_hbm, gain1), (w1_hbm, w1), (wd_hbm, wd),
            (gain2_hbm, gain2), (w2_hbm, w2), (shortcut_hbm, shortcut)))]
    for one in loads:
        one.start()

    def remote(src, dst, index, who):
        return pltpu.make_async_remote_copy(
            src_ref=src, dst_ref=dst, send_sem=near_send.at[index], recv_sem=near_recv.at[index],
            device_id=who, device_id_type=MESH)

    frames = remote(video_hbm.at[2:4], past_video, 0, after)
    ups = [remote(part_out.at[0, n], part_in.at[0, n], 1 + n, up) for n in range(2)]
    downs = [remote(part_out.at[1, n], part_in.at[1, n], 3 + n, down) for n in range(2)]
    later = remote(windows.at[1, 4:6], windows.at[1, 0:2], 5, after)

    def when(condition, *steps):
        @pl.when(condition)
        def _():
            for step in steps:
                step()

    ones1[...] = jnp.where(
        iota2((768, 384), 0) % 384 // 96 == iota2((768, 384), 1) // 96, 1.0, 0.0).astype(BF16)
    line = iota2((128, 128), 0)
    order = jnp.where(
        iota2((128, 128), 1) == jnp.where(line < 64, 2 * line, 2 * line - 127), 1.0, 0.0).astype(BF16)
    loads[1].wait()
    gain_lanes1 = 0.5 * place_exact(
        gain1[...], jnp.where(iota2((96, 384), 1) % 96 == iota2((96, 384), 0), 1.0, 0.0).astype(BF16))
    loads[0].wait()

    lane64 = iota2((64, 128), 1)
    line64 = iota2((64, 128), 0)

    def windows_of(even, odd):
        return shift_up(even[:, 0:128]), shift_up(even[:, 128:256]), shift_down(odd[:, 256:384])

    def spread_first(t, r, even, odd):
        after0, after1, before2 = windows_of(even, odd)
        last = jnp.where(line64 == 63, pltpu.roll(odd[:, 256:384], 32, 1), 0.0)
        cells1[t, r, 0] = jnp.concatenate([
            even, odd[:, 0:128], jnp.where(lane64 < 64, odd[:, 128:256], 0.0),
            jnp.where(lane64 < 32, 0.0, before2)], 1).astype(BF16)
        cells1[t, r, 1] = jnp.concatenate([
            odd, after0, jnp.where(lane64 < 64, after1, last),
            jnp.where(lane64 < 32, last, even[:, 256:384])], 1).astype(BF16)

    def norm_first(t, source, f):
        values = jnp.concatenate([dot(order, source[f, 0]), dot(order, source[f, 1])], 0)
        meansq = dot(squares_split(values), ones1[...]) * (1.0 / 96.0)
        result = normsilu(values, meansq, gain_lanes1)
        for r in range(2):
            even, odd = result[128 * r:128 * r + 64], result[128 * r + 64:128 * r + 128]
            spread_first(t, r, even, odd)
        return values

    def norm_own(t):
        values = norm_first(t + 2, video, t)
        for r in range(2):
            even, odd = values[128 * r:128 * r + 64], values[128 * r + 64:128 * r + 128]
            cellsv[t, r, 0] = jnp.concatenate([even, odd[:, 0:128]], 1).astype(BF16)
            cellsv[t, r, 1] = jnp.concatenate([odd, shift_up(even[:, 0:128])], 1).astype(BF16)

    for t in range(4):
        norm_own(t)

    count = has_up.astype(jnp.int32) + has_down.astype(jnp.int32) + has_past.astype(jnp.int32) + has_next.astype(jnp.int32)
    pl.semaphore_wait(barrier, count + (z_total - 1) + (square - 1))
    when(has_next, frames.start)

    @pl.when(jnp.logical_not(has_up))
    def _():
        part_in[1] = jnp.zeros((2, 128, 384), BF16)

    @pl.when(jnp.logical_not(has_down))
    def _():
        part_in[0] = jnp.zeros((2, 128, 384), BF16)

    @pl.when(jnp.logical_not(has_past))
    def _():
        past_video[...] = jnp.zeros((2, 2, 128, 384), BF16)
        windows[1, 0:2] = jnp.zeros((2, 64, 640), BF16)

    loads[3].wait()
    wdp[...] = jnp.zeros((96, 1152), BF16)
    for i in range(3):
        for j in range(3):
            wdp[:, 128 * (3 * i + j):128 * (3 * i + j) + 96] = wd[i, 96 * j:96 * j + 96]
    blank = jnp.zeros((96, 128), F32)

    def down_tap(i, j):
        return wdp[:, 128 * (3 * i + j):128 * (3 * i + j) + 128]

    for r, i in ((1, 0), (2, 1), (3, 2)):
        none = blank.astype(BF16)
        for n, (q0, q1) in enumerate((
                (down_tap(i, 0), none), (down_tap(i, 1), none), (down_tap(i, 2), down_tap(i, 0)),
                (none, down_tap(i, 1)), (none, down_tap(i, 2)))):
            w5[r, 2304 + 96 * n:2400 + 96 * n] = jnp.concatenate([q0, q1], 1)
        w5[r, 2784:2816] = jnp.zeros((32, 256), BF16)
    below = has_down.astype(F32)
    loads[2].wait()

    def compose_step(a, carry):
        for i in range(3):
            products[i] = dot(w1[3 * a + i], wdp[...])

        def total(r, pairs):
            result = None
            for i in range(3):
                lower = r - i
                if 0 <= lower <= 2:
                    for j, across in pairs:
                        lane = 128 * (3 * lower + across)
                        term = products[i, 96 * j:96 * j + 96, lane:lane + 128]
                        if r == 2 and lower == 2:
                            term = term * below
                        result = term if result is None else result + term
            return result

        start = a * 768
        for r in range(5):
            at = [total(r, [(j, c - j) for j in range(3) if 0 <= c - j <= 2]) for c in range(5)]
            beyond = -total(r, [(0, 2)])
            for n, (q0, q1) in enumerate((
                    (at[1], blank), (at[2], at[0]), (at[3], at[1]), (at[4], at[2]),
                    (blank, at[3]), (blank, at[4]), (blank, beyond), (at[0], blank))):
                w5[r, pl.ds(start + 96 * n, 96)] = jnp.concatenate([q0, q1], 1).astype(BF16)
        return carry

    for a in range(3):
        compose_step(a, 0)

    def row_cells(t, r, with_video):
        pieces = [cells1[t + a:t + a + 2, r].reshape(256, 768) for a in range(3)]
        if with_video:
            pieces.append(cellsv[t:t + 2, r].reshape(256, 512))
        return jnp.concatenate(pieces, 1)

    def compact(total):
        frames_here = []
        for f in range(2):
            base = 128 * f
            frames_here.append(packed([
                total[base + 64 * p:base + 64 * p + 64, 128 * q:128 * q + 128]
                for p in range(2) for q in range(2)]))
        return jnp.concatenate(frames_here, 0)

    def send_partials(half, t):
        total = dot(row_cells(t, 0, True), w5[3]) + dot(row_cells(t, 1, False), w5[4, 0:2304])
        part_out[0, half] = compact(total).astype(BF16)
        when(has_up, ups[half].start)
        part_out[1, half] = compact(dot(row_cells(t, 1, False), w5[0, 0:2304])).astype(BF16)
        when(has_down, downs[half].start)

    def sum_own(half, t):
        total = dot(row_cells(t, 0, True), w5[1]) + dot(row_cells(t, 1, True), w5[2])
        own_sum[half] = compact(total)

    def reduce_half(half):
        when(has_down, ups[half].wait_recv)
        when(has_up, downs[half].wait_recv)
        total = own_sum[half] + part_in[0, half].astype(F32) + part_in[1, half].astype(F32)
        total = total.astype(BF16).astype(F32)
        spot_in_block = iota2((64, 128), 0) % 8
        wide = []
        for f in range(2):
            cell = total[64 * f:64 * f + 64]
            edge = jnp.where(spot_in_block < 4, shift_down(cell[:, 256:384]), shift_up(cell[:, 0:128]))
            wide.append(jnp.concatenate([cell, edge], 1).reshape(z_total, 8, 512))
        z_out[half] = jnp.concatenate(wide, 1).astype(BF16)

    def z_copy(half, step, arriving):
        other, who = z_partner(step)
        here = (z - step + z_total) % z_total
        slot = half * z_total + step
        return pltpu.make_async_remote_copy(
            src_ref=z_out.at[half, other], dst_ref=z_in.at[half, here if arriving else z],
            send_sem=z_send.at[slot], recv_sem=z_recv.at[slot], device_id=who, device_id_type=MESH)

    def send_z(half):
        for step in sorted(range(1, z_total), key=lambda step: -min(step, z_total - step)):
            z_copy(half, step, False).start()
        z_in[half, z] = z_out[half, z]

    send_partials(0, 2)
    sum_own(0, 2)

    def halo_frames():
        frames.wait_recv()

    when(has_past, halo_frames)
    for t in range(2):
        norm_first(t, past_video, t)
    send_partials(1, 0)
    reduce_half(0)
    send_z(0)
    sum_own(1, 0)

    lane2 = iota2((192, 768), 1)
    source2 = iota2((192, 768), 0)
    places2 = jnp.where(lane2 == jnp.where(lane2 < 384, source2, source2 + 576), 1.0, 0.0).astype(BF16)
    loads[5].wait()

    def weight2_step(tap, carry):
        placed = dot(w2[tap], places2)
        p0, p1 = placed[:, 0:384], placed[:, 384:768]
        wa2[tap, 0:96] = (p0[96:192] + p1[0:96]).astype(BF16)
        wa2[tap, 96:192] = (p0[192:288] + p1[96:192]).astype(BF16)
        wa2[tap, 192:288] = p1[192:288].astype(BF16)
        wa2[tap, 288:384] = p0[0:96].astype(BF16)
        wb2[tap, 0:96] = p1[192:288].astype(BF16)
        wb2[tap, 96:192] = p0[0:96].astype(BF16)
        wb2[tap, 192:288] = (p0[96:192] + p1[0:96]).astype(BF16)
        wb2[tap, 288:384] = (p0[192:288] + p1[96:192]).astype(BF16)
        return carry

    lax.fori_loop(0, 9, weight2_step, 0)

    loads[6].wait()
    placed2 = dot(shortcut[...], places2).astype(BF16)
    wsa[0:96] = placed2[:, 0:384]
    wsa[96:192] = placed2[:, 384:768]
    wsa[192:384] = jnp.zeros((192, 384), BF16)
    wsb[0:192] = jnp.zeros((192, 384), BF16)
    wsb[192:288] = placed2[:, 0:384]
    wsb[288:384] = placed2[:, 384:768]
    rows640 = iota2((640, 640), 0)
    twice = jnp.logical_or(jnp.logical_and(rows640 >= 384, rows640 < 416), rows640 >= 608)
    from_group = jnp.where(twice, -1, group_of(rows640))
    same = jnp.where(from_group == group_of(iota2((640, 640), 1)), 1.0, 0.0).astype(BF16)
    ones2[0:640] = same
    ones2[640:1280] = same
    loads[4].wait()
    gain_lanes2[...] = jnp.broadcast_to(0.5 * place_exact(gain2[...], jnp.where(
        channel_of(iota2((96, 640), 1)) == iota2((96, 640), 0), 1.0, 0.0).astype(BF16)), (8, 640))

    reduce_half(1)
    send_z(1)

    def yc_copy(half, step, arriving):
        other, who = square_partner(step)
        here = (spot - step + square) % square
        slot = half * square + step
        return pltpu.make_async_remote_copy(
            src_ref=yc_out.at[half, other], dst_ref=yc_in.at[half, here if arriving else spot],
            send_sem=yc_send.at[slot], recv_sem=yc_recv.at[slot], device_id=who, device_id_type=MESH)

    lane8 = iota2((8, 128), 1)
    line8 = iota2((8, 128), 0)

    def relay(half):
        for turn in range(z_total):
            source = (z - turn + z_total) % z_total
            if turn:
                z_copy(half, turn, True).wait_recv()
            cells = z_in[half, source].astype(F32)
            for f in range(2):
                cell = cells[8 * f:8 * f + 8]
                t0, t1, t2, edge = (cell[:, 128 * n:128 * n + 128] for n in range(4))
                before = jnp.where(line8 == 0, edge, pltpu.roll(t2, 1, 0))
                following = jnp.where(line8 == 7, edge, pltpu.roll(t0, 7, 0))
                parts = (t0, t1, t2, jnp.where(lane8 < 32, t2, before), jnp.where(lane8 < 96, following, t0))
                for n, part in enumerate(parts):
                    yc_wide[n, pl.ds(f * 8 + source, 8, stride=16), :] = part
        for n in range(5):
            yc_out[half, :, :, 128 * n:128 * n + 128] = yc_wide[n].astype(BF16).reshape(8, 16, 128)
        for step in sorted(range(1, square), key=lambda step: -min(step, square - step)):
            yc_copy(half, step, False).start()
        yc_in[half, spot] = yc_out[half, spot]

    relay(0)
    relay(1)

    def norm_second(half, t):
        for turn in range(square):
            source = (spot - turn + square) % square
            if turn:
                yc_copy(half, turn, True).wait_recv()
            cells = yc_in[half, source].astype(F32)
            start = (source % clip_total) * row_total + source // clip_total
            for f in range(2):
                for n in range(5):
                    tiles[n, pl.ds(64 * f + start, 8, stride=y_total), :] = cells[8 * f:8 * f + 8, 128 * n:128 * n + 128]
        values = jnp.concatenate([tiles[n] for n in range(5)], 1)
        raw[t:t + 2] = values[:, 0:384].astype(BF16).reshape(2, 64, 384)
        meansq = dot(squares_split(values), ones2[...]) * (1.0 / 96.0)
        second = normsilu(values, meansq, gain_lanes2[0:1])
        windows[1, t + 2:t + 4] = second.astype(BF16).reshape(2, 64, 640)
        return second

    def shifted(second, t):
        line = iota2((128, 640), 0) % 32
        windows[0, t:t + 2] = jnp.where(line == 0, 0.0, pltpu.roll(second, 1, 0)).astype(BF16).reshape(2, 64, 640)
        windows[2, t:t + 2] = jnp.where(line == 31, 0.0, pltpu.roll(second, 127, 0)).astype(BF16).reshape(2, 64, 640)

    second = norm_second(0, 2)
    when(has_next, later.start)
    shifted(second, 4)
    second = norm_second(1, 0)
    shifted(second, 2)
    when(has_past, later.wait_recv)
    shifted(windows[1, 0:2].reshape(128, 640).astype(F32), 0)

    def conv(weights, direct, lane_sets):
        acc = dot(raw[...].reshape(256, 384), direct[...])
        for a in range(3):
            pieces = []
            for i in range(3):
                pieces += [windows[i, a:a + 4, :, lo:hi].reshape(256, hi - lo) for lo, hi in lane_sets]
            acc += dot(jnp.concatenate(pieces, 1), weights[3 * a:3 * a + 3].reshape(1152, 384))
        return acc.astype(BF16).reshape(4, 2, 32, 384)

    left = conv(wa2, wsa, ((0, 256), (384, 512)))
    for c in range(2):
        out[c, :, :, 0:384] = left[:, c]
    right = conv(wb2, wsb, ((512, 640), (128, 384)))
    for c in range(2):
        out[c, :, :, 384:768] = right[:, c]

    when(has_up, ups[0].wait_send, ups[1].wait_send)
    when(has_down, downs[0].wait_send, downs[1].wait_send)
    when(has_next, frames.wait_send, later.wait_send)
    for half in range(2):
        for step in range(1, z_total):
            z_copy(half, step, False).wait_send()
        for step in range(1, square):
            yc_copy(half, step, False).wait_send()


def vmem(shape, dtype=BF16):
    return pltpu.VMEM(shape, dtype)


def shards(sizes, video, gain_first, conv_first, down, gain_second, conv_second, shortcut):
    dma = pltpu.SemaphoreType.DMA
    latents = pl.pallas_call(
        functools.partial(encoder_kernel, sizes),
        out_shape=jax.ShapeDtypeStruct((2, 4, 32, 768), BF16),
        in_specs=[pl.BlockSpec(memory_space=pl.ANY)] * 7,
        out_specs=pl.BlockSpec(memory_space=pltpu.VMEM),
        scratch_shapes=[
            vmem((4, 2, 128, 384)), vmem((1, 96), F32), vmem((9, 288, 96)), vmem((3, 288, 96)),
            vmem((1, 96), F32), vmem((9, 288, 192)), vmem((96, 192)),
            vmem((768, 384)), vmem((1280, 640)), vmem((8, 640), F32),
            vmem((2, 2, 128, 384)), vmem((6, 2, 2, 64, 768)), vmem((4, 2, 2, 64, 512)),
            vmem((96, 1152)), vmem((3, 288, 1152), F32), vmem((5, 2816, 256)),
            vmem((2, 2, 128, 384)), vmem((2, 2, 128, 384)), vmem((2, 128, 384), F32),
            vmem((2, 8, 16, 512)), vmem((2, 8, 16, 512)),
            vmem((5, 128, 128), F32), vmem((2, 8, 16, 640)), vmem((2, 8, 16, 640)),
            vmem((5, 128, 128), F32), vmem((3, 6, 64, 640)), vmem((4, 64, 384)),
            vmem((9, 384, 384)), vmem((9, 384, 384)), vmem((384, 384)), vmem((384, 384)),
            dma((6,)), dma((6,)), dma((16,)), dma((16,)), dma((16,)), dma((16,)), dma((7,)),
        ],
        compiler_params=pltpu.CompilerParams(
            collective_id=0, has_side_effects=True, vmem_limit_bytes=VMEM_LIMIT),
        name="encoder",
    )(
        video.reshape(4, 2, 128, 384), gain_first.reshape(1, 96),
        conv_first.reshape(9, 288, 96), down.reshape(3, 288, 96),
        gain_second.reshape(1, 96), conv_second.reshape(9, 288, 192), shortcut,
    )
    return latents.reshape(2, 4, 32, 1, 768)


def solution(mesh):
    sizes = (mesh.shape["rows"], mesh.shape["tm"], mesh.shape["clip"], 8)
    return jax.shard_map(
        functools.partial(shards, sizes),
        mesh=mesh,
        in_specs=(P("clip", "tm", "rows", None, None), P(), P(), P(), P(), P(), P()),
        out_specs=P(None, "tm", None, ("rows", "clip"), None),
        check_vma=False,
    )
```
